32 devices in a mesh: dp: 1, seq: 32 (over z, y, x, core).
Axes of the slice: x: 2, y: 2, z: 4, core: 2. Of those that a mesh axis runs over, the one named last changes fastest.
Arguments:
- queries: bfloat16 [1, 8192, 1024], P('dp', 'seq'), may hold values from -8 to 8
- keys: bfloat16 [1, 8192, 1024], P('dp', 'seq'), may hold values from -8 to 8
- values: bfloat16 [1, 8192, 1024], P('dp', 'seq'), may hold values from -12 to 12
- out_weight: bfloat16 [1024, 2048], P('seq', 'dp'), may hold values from -0.1875 to 0.1875
- out_grad: bfloat16 [1, 8192, 2048], P('dp', 'seq'), may hold values from -6 to 6
Outputs:
- attended: bfloat16 [1, 8192, 2048], P('dp', 'seq')
- grad_queries: bfloat16 [1, 8192, 1024], P('dp', 'seq')
- grad_keys: bfloat16 [1, 8192, 1024], P('dp', 'seq')
- grad_values: bfloat16 [1, 8192, 1024], P('dp', 'seq')
- grad_out_weight: float32 [1024, 2048], P('seq', 'dp')
The draws below stay inside these ranges and needn't reach their ends.
All inputs are finite; a program needn't handle non-finite values.
Results may differ from the reference program's by a relative error of at most 0.029.
Values may be sent and summed in bfloat16 or wider, within the bound.
No kernel may reach another device: no remote copies, remote signals or barrier semaphores. Data moves between devices by JAX's collectives and lax.ppermute only.
A program may use at most 128 MiB of HBM per device.

```python
import math
import jax
import jax.numpy as jnp
from jax import lax

D = 2048
HEADS = 8
HS = 128
NR = 128
HD = 1024
BATCH = 1
TOKENS = 8192


def draw_queries(key, part):
    base_draw = 2.0 * jax.random.normal(jax.random.fold_in(key, 1), (BATCH, TOKENS, HEADS * HS), jnp.float32)
    return jnp.clip(base_draw, -8.0, 8.0).astype(jnp.bfloat16)


def draw_keys(key, part):
    base_draw = jax.random.normal(jax.random.fold_in(key, 3), (BATCH, TOKENS, HEADS * HS), jnp.float32)
    return jnp.clip(base_draw, -8.0, 8.0).astype(jnp.bfloat16)


def strengthened(values, own_key, source, target, parts, factor):
    owner, partner = [(jnp.arange(values.shape[dim]) // (values.shape[dim] // parts)).reshape([-1 if axis == dim else 1 for axis in range(values.ndim)]) for dim in (source, target)]
    chosen = jax.random.permutation(own_key, parts)[partner]
    strong = (owner == chosen) | (owner == (partner + parts // 2) % parts)
    return jnp.where(strong, factor * values, values)


def block_levels(key, dims, shards, smallest, top_value):
    def one(position, parts):
        heights = jax.random.uniform(jax.random.fold_in(jax.random.fold_in(key, 6), position), (parts,), jnp.float32, smallest / len(shards), top_value / len(shards))
        return jnp.repeat(jnp.exp(heights), dims[position] // parts).reshape((-1,) + (1,) * (len(dims) - position - 1))

    loudness = one(*shards[0])
    for cut in shards[1:]:
        loudness = loudness * one(*cut)
    return loudness


def centred(rng, dims, deviation, limit, cuts=(), kind=jnp.bfloat16):
    level = block_levels(rng, dims, cuts, -0.22, 0.18) if cuts else 1.0
    entries = jax.random.normal(rng, dims, jnp.float32) * deviation * level
    return jnp.minimum(jnp.maximum(entries, -limit), limit).astype(kind)


def gaussian_with(key, dims, scale, limit, cuts, heavy, dtype=jnp.bfloat16):
    array = scale * jax.random.normal(key, dims, jnp.float32)
    if cuts:
        array = array * block_levels(key, dims, cuts, -0.22, 0.18)
    return jnp.clip(strengthened(array, jax.random.fold_in(key, 3), *heavy), -limit, limit).astype(dtype)


def setup_inputs(seed: int = 0) -> dict:
    streams_of = jax.random.split(jax.random.key(seed), 6)
    queries = draw_queries(jax.random.fold_in(streams_of[5], 71), 0)
    keys = draw_keys(jax.random.fold_in(streams_of[5], 71), 0)
    values = centred(streams_of[2], (BATCH, TOKENS, HD), 2.0, 12.0, ((1, 32),))
    out_weight = centred(streams_of[3], (HD, D), HD ** -0.5, 0.1875, ((0, 32),))
    out_grad = gaussian_with(streams_of[4], (BATCH, TOKENS, D), 1.0, 6.0, ((1, 32),), (1, 2, 32, 2.75))
    return {"queries": queries, "keys": keys, "values": values, "out_weight": out_weight, "out_grad": out_grad}


HALF_ROOT = 0.7071067811865476

def pool_pairs(row_data):
    shaped = row_data.astype(jnp.float32).reshape(row_data.shape[0] // 2, 2, row_data.shape[1])
    return ((shaped[:, 0] + shaped[:, 1]) * HALF_ROOT).astype(jnp.bfloat16)

def unpool_pairs(grad_data):
    spread = grad_data * HALF_ROOT
    return jnp.broadcast_to(spread[:, None, :], (spread.shape[0], 2, spread.shape[1])).reshape(2 * spread.shape[0], spread.shape[1])

def add_rows(target_array, update_rows, row_start):
    current = lax.dynamic_slice_in_dim(target_array, row_start, update_rows.shape[0], 0)
    return lax.dynamic_update_slice_in_dim(target_array, current + update_rows, row_start, 0)

def one_sequence(query_rows, key_rows, value_rows, grad_rows, out_weight):
    blocks_all = TOKENS // NR
    levels = blocks_all.bit_length() - 1
    inner_width = HEADS * HS
    score_scale = 1.0 / math.sqrt(HS)
    pair_rows = jnp.concatenate([key_rows, value_rows], axis=1)
    coarse = [pair_rows]
    for height in range(levels - 1):
        coarse.append(pool_pairs(coarse[-1]))
    d_attn = jnp.dot(grad_rows, out_weight.T, preferred_element_type=jnp.float32).astype(jnp.bfloat16)

    def step_block(block_index, carry):
        attn_rows, grad_query, coarse_grads = carry
        row_start = (block_index * NR).astype(jnp.int32)
        starts = []
        for height in range(levels):
            group_index = block_index // 2 ** height
            starts.append(((group_index + 1 - 2 * (group_index % 2)) * NR).astype(jnp.int32))
        pieces = [lax.dynamic_slice_in_dim(coarse[0], row_start, NR, 0)]
        for height in range(levels):
            pieces.append(lax.dynamic_slice_in_dim(coarse[height], starts[height], NR, 0))
        key_set = jnp.concatenate(pieces, axis=0).astype(jnp.float32)
        key_heads = key_set[:, :inner_width].reshape(-1, HEADS, HS)
        value_heads = key_set[:, inner_width:].reshape(-1, HEADS, HS)
        query_block = lax.dynamic_slice_in_dim(query_rows, row_start, NR, 0).astype(jnp.float32).reshape(NR, HEADS, HS)
        grad_block = lax.dynamic_slice_in_dim(d_attn, row_start, NR, 0).astype(jnp.float32).reshape(NR, HEADS, HS)
        scores = jnp.einsum('qhd,khd->hqk', query_block, key_heads) * score_scale
        top_score = lax.optimization_barrier(jnp.max(scores, axis=-1, keepdims=True))
        exp_scores = jnp.exp(scores - top_score)
        probs_full = exp_scores / lax.optimization_barrier(jnp.sum(exp_scores, axis=-1, keepdims=True))
        probs_low = lax.optimization_barrier(probs_full.astype(jnp.bfloat16)).astype(jnp.float32)
        out_block = jnp.einsum('hqk,khd->qhd', probs_low, value_heads).reshape(NR, inner_width).astype(jnp.bfloat16)
        dprob = jnp.einsum('qhd,khd->hqk', grad_block, value_heads)
        center = lax.optimization_barrier(jnp.sum(probs_full * dprob, axis=-1, keepdims=True))
        dscore = lax.optimization_barrier((probs_full * (dprob - center) * score_scale).astype(jnp.bfloat16)).astype(jnp.float32)
        dquery = jnp.einsum('hqk,khd->qhd', dscore, key_heads).reshape(NR, inner_width)
        dkey = jnp.einsum('hqk,qhd->khd', dscore, query_block).reshape(-1, inner_width)
        dvalue = jnp.einsum('hqk,qhd->khd', probs_low, grad_block).reshape(-1, inner_width)
        dpair = jnp.concatenate([dkey, dvalue], axis=1)
        attn_rows = lax.dynamic_update_slice_in_dim(attn_rows, out_block, row_start, 0)
        grad_query = lax.dynamic_update_slice_in_dim(grad_query, dquery, row_start, 0)
        new_grads = list(coarse_grads)
        new_grads[0] = add_rows(new_grads[0], dpair[:NR], row_start)
        for height in range(levels):
            new_grads[height] = add_rows(new_grads[height], dpair[(height + 1) * NR:(height + 2) * NR], starts[height])
        return (attn_rows, grad_query, tuple(new_grads))
    initial = (jnp.zeros((TOKENS, inner_width), jnp.bfloat16), jnp.zeros((TOKENS, inner_width), jnp.float32), tuple((jnp.zeros(entry.shape, jnp.float32) for entry in coarse)))
    attn_rows, grad_query, coarse_grads = lax.fori_loop(0, blocks_all, step_block, initial)
    coarse_grads = list(coarse_grads)
    for height in reversed(range(1, levels)):
        coarse_grads[height - 1] = coarse_grads[height - 1] + unpool_pairs(coarse_grads[height])
    attended = jnp.dot(attn_rows, out_weight, preferred_element_type=jnp.float32).astype(jnp.bfloat16)
    weight_part = jnp.dot(attn_rows.T, grad_rows, preferred_element_type=jnp.float32)
    pair_grad = coarse_grads[0]
    return (attended, grad_query.astype(jnp.bfloat16), pair_grad[:, :inner_width].astype(jnp.bfloat16), pair_grad[:, inner_width:].astype(jnp.bfloat16), weight_part)

def reference(queries, keys, values, out_weight, out_grad):

    def per_sequence(sequence_items):
        return one_sequence(sequence_items[0], sequence_items[1], sequence_items[2], sequence_items[3], out_weight)
    attended, grad_queries, grad_keys, grad_values, weight_parts = lax.map(per_sequence, (queries, keys, values, out_grad))
    grad_out_weight = lax.optimization_barrier(jnp.sum(weight_parts, axis=0)) * (1.0 / math.sqrt(BATCH * TOKENS))
    return (attended, grad_queries, grad_keys, grad_values, grad_out_weight)
```

```python
import math

import jax
import jax.numpy as jnp
from jax import lax
from jax.experimental import pallas as pl
from jax.experimental.pallas import tpu as pltpu
from jax.sharding import PartitionSpec as P

HEADS = 8
HS = 128
NR = 128

HALF_ROOT = 0.7071067811865476
SCORE_SCALE = 1.0 / math.sqrt(HS)
EXP2_SCALE = SCORE_SCALE * math.log2(math.e)
F32 = jnp.float32
BF16 = jnp.bfloat16
VMEM_LIMIT = 40 * 1024 * 1024


def permute(value, masks):
    count = lax.axis_size("seq")
    return lax.ppermute(value, "seq", [(i, i ^ masks[i & 1]) for i in range(count)])


def swap(value, mask):
    return permute(value, (mask, mask))


def call(body, meta, operands, specs, shapes, out_specs, scratch=(), grid=(1,), flops=0):
    moved = sum(math.prod(o.shape) * o.dtype.itemsize for o in operands)
    moved += sum(math.prod(s.shape) * s.dtype.itemsize for s in jax.tree.leaves(shapes))
    return pl.pallas_call(
        body,
        grid_spec=pltpu.PrefetchScalarGridSpec(
            num_scalar_prefetch=1,
            grid=grid,
            in_specs=specs,
            out_specs=out_specs,
            scratch_shapes=list(scratch),
        ),
        out_shape=shapes,
        compiler_params=pltpu.CompilerParams(vmem_limit_bytes=VMEM_LIMIT),
        cost_estimate=pl.CostEstimate(flops=flops, bytes_accessed=moved, transcendentals=0),
    )(meta, *operands)


def whole(array):
    return pl.BlockSpec(array.shape, lambda i, m: (0,) * len(array.shape))


def own_half(array):
    return pl.BlockSpec((array.shape[0], array.shape[1] // 2), lambda i, m: (0, m[0]))


def struct(rows, cols, dtype):
    return jax.ShapeDtypeStruct((rows, cols), dtype)


def dot(a, b, dims):
    return lax.dot_general(a, b, (dims, ((), ())), preferred_element_type=F32)


NN = ((1,), (0,))
NT = ((1,), (1,))
TN = ((0,), (0,))


def group_matrix(rows, cols, row_div, col_div):
    row = lax.broadcasted_iota(jnp.int32, (rows, cols), 0) // row_div
    col = lax.broadcasted_iota(jnp.int32, (rows, cols), 1) // col_div
    return jnp.where(row == col, 1.0, 0.0).astype(BF16)


def pool(rows):
    half = rows.shape[0] // 2
    return (dot(group_matrix(half, 2 * half, 1, 2), rows, NN) * HALF_ROOT).astype(BF16)


def spread(grad, times, factor):
    high = grad.astype(BF16)
    low = (grad - high.astype(F32)).astype(BF16)
    matrix = group_matrix(times * grad.shape[0], grad.shape[0], times, 1)
    return (dot(matrix, high, NN) + dot(matrix, low, NN)) * factor


def pool_body(meta, keys, values, other, *outs):
    own = jnp.concatenate([keys[...], values[...]], axis=1)
    first_own = pool(own)
    first_other = pool(other[...])
    outs[0][...] = first_own
    outs[1][...] = first_other
    rows = jnp.concatenate([pool(first_own), pool(first_other)], axis=0)
    outs[2][...] = rows
    for out in outs[3:]:
        rows = pool(rows)
        out[...] = rows


def forward_body(heads, n_far, meta, q_own, q_other, k_own, v_own, k_other, v_other, *refs):
    near_k = (k_own, k_other)
    near_v = (v_own, v_other)
    next_k = refs[0:2]
    next_v = refs[2:4]
    far_k_refs = refs[4 : 4 + n_far]
    far_v_refs = refs[4 + n_far : 4 + 2 * n_far]
    attn_ref, probs_ref = refs[4 + 2 * n_far :]
    for head in range(heads):
        at = slice(head * HS, (head + 1) * HS)
        far_k = [ref[:, at] for ref in far_k_refs]
        far_v = [ref[:, at] for ref in far_v_refs]
        for group, q_ref in enumerate((q_own, q_other)):
            length = q_ref.shape[0]
            key = jnp.concatenate([near_k[group][:, at], next_k[group][:, at]] + far_k, axis=0)
            value = jnp.concatenate([near_v[group][:, at], next_v[group][:, at]] + far_v, axis=0)
            scores = dot(key, q_ref[:, at], NT)
            top = jnp.max(scores, axis=0, keepdims=True)
            weights = jnp.exp2((scores - top) * EXP2_SCALE)
            total = jnp.sum(weights, axis=0, keepdims=True)
            probs = (weights * (1.0 / total)).astype(BF16)
            probs_ref[2 * head + group] = probs
            attn = dot(value, probs, TN)
            attn_ref[at, group * length : (group + 1) * length] = attn.astype(BF16)


def backward_body(
    heads, n_far, meta, q_own, q_other, k_own, v_own, k_other, v_other, d_keep, d_recv, probs_ref, *refs
):
    near_k = (k_own, k_other)
    near_v = (v_own, v_other)
    next_k = refs[0:2]
    next_v = refs[2:4]
    far_k_refs = refs[4 : 4 + n_far]
    far_v_refs = refs[4 + n_far : 4 + 2 * n_far]
    refs = refs[4 + 2 * n_far :]
    dq_refs = refs[0:2]
    near_dk = refs[2:4]
    near_dv = refs[4:6]
    far_dk = refs[6 : 6 + n_far]
    far_dv = refs[6 + n_far : 6 + 2 * n_far]
    near = near_k[0].shape[0]
    after = near + next_k[0].shape[0]
    for head in range(heads):
        at = slice(head * HS, (head + 1) * HS)
        far_k = [ref[:, at] for ref in far_k_refs]
        far_v = [ref[:, at] for ref in far_v_refs]
        dks = []
        dvs = []
        for group, q_ref in enumerate((q_own, q_other)):
            length = q_ref.shape[0]
            rows = slice(group * length, (group + 1) * length)
            query = q_ref[:, at]
            key = jnp.concatenate([near_k[group][:, at], next_k[group][:, at]] + far_k, axis=0)
            value = jnp.concatenate([near_v[group][:, at], next_v[group][:, at]] + far_v, axis=0)
            d_attn = (d_keep[rows, at] + d_recv[rows, at].astype(F32)).astype(BF16)
            probs_low = probs_ref[2 * head + group]
            probs = probs_low.astype(F32)
            d_prob = dot(value, d_attn, NT)
            center = jnp.sum(probs * d_prob, axis=0, keepdims=True)
            d_score = (probs * (d_prob - center)).astype(BF16)
            dq = dot(key, d_score, TN) * SCORE_SCALE
            dq_refs[group][:, at] = dq.T.astype(BF16)
            dks.append(dot(d_score, query, NN) * SCORE_SCALE)
            dvs.append(dot(probs_low, d_attn, NN))
        for grads, near_out, far_out in ((dks, near_dk, far_dk), (dvs, near_dv, far_dv)):
            for group in range(2):
                total = grads[group][:near] + spread(grads[1 - group][near:after], 2, HALF_ROOT)
                near_out[group][:, at] = total.astype(near_out[group].dtype)
            far = grads[0][after:] + grads[1][after:]
            start = 0
            for out in far_out:
                out[:, at] = far[start : start + out.shape[0]].astype(BF16)
                start += out.shape[0]


def ordered_weight(meta, first, second, scratch, piece):
    half = first.shape[0] // piece
    for index in range(2 * half):
        source = first if index < half else second
        start = (index % half) * piece
        place = pl.multiple_of(meta[1 + index] * piece, piece)
        scratch[pl.ds(place, piece), :] = source[start : start + piece, :]


def d_attn_body(piece, meta, grad_own, grad_other, first, second, keep, send, scratch):
    ordered_weight(meta, first, second, scratch, piece)
    length = grad_own.shape[0]
    width = keep.shape[1]
    mine = scratch[pl.ds(pl.multiple_of(meta[0] * width, width), width), :]
    theirs = scratch[pl.ds(pl.multiple_of((1 - meta[0]) * width, width), width), :]
    send[:length] = dot(grad_other[...], theirs, NT).astype(BF16)
    send[length:] = dot(grad_own[...], theirs, NT).astype(BF16)
    keep[:length] = dot(grad_own[...], mine, NT)
    keep[length:] = dot(grad_other[...], mine, NT)


def attended_body(piece, meta, attn_mine, attn_theirs, first, second, keep, send, scratch):
    ordered_weight(meta, first, second, scratch, piece)
    length = keep.shape[0]
    width = attn_mine.shape[0]
    mine = scratch[pl.ds(pl.multiple_of(meta[0] * width, width), width), :]
    theirs = scratch[pl.ds(pl.multiple_of((1 - meta[0]) * width, width), width), :]
    send[...] = (
        dot(attn_mine[:, length:], mine, TN) + dot(attn_theirs[:, :length], theirs, TN)
    ).astype(BF16)
    keep[...] = (
        dot(attn_mine[:, :length], mine, TN) + dot(attn_theirs[:, length:], theirs, TN)
    ).astype(BF16)


def weight_grad_body(piece, meta, attn_mine, attn_theirs, grad_own, grad_other, keep, send, scratch):
    length = grad_own.shape[0]
    width = attn_mine.shape[0]
    mine = dot(attn_mine[:, :length], grad_own[...], NN) + dot(
        attn_mine[:, length:], grad_other[...], NN
    )
    scratch[pl.ds(pl.multiple_of(meta[0] * width, width), width), :] = mine.astype(BF16)
    theirs = dot(attn_theirs[:, length:], grad_own[...], NN) + dot(
        attn_theirs[:, :length], grad_other[...], NN
    )
    scratch[pl.ds(pl.multiple_of((1 - meta[0]) * width, width), width), :] = theirs.astype(BF16)
    half = keep.shape[0] // piece
    for index in range(2 * half):
        target = keep if index < half else send
        start = (index % half) * piece
        place = pl.multiple_of(meta[1 + index] * piece, piece)
        target[start : start + piece, :] = scratch[pl.ds(place, piece), :]


def cascade_body(counts, meta, *refs):
    total = None
    start = 0
    for count in counts:
        level = refs[start][...].astype(F32)
        for ref in refs[start + 1 : start + count]:
            level = level + ref[...].astype(F32)
        start += count
        total = level if total is None else level + spread(total, 2, HALF_ROOT)
    keep, send = refs[start:]
    half = keep.shape[0]
    keep[...] = total[:half]
    send[...] = total[half:].astype(BF16)


def finish_body(meta, dk_keep, dv_keep, dk_recv, dv_recv, up_keep, up_recv, dk, dv):
    width = dk_keep.shape[1]
    times = dk_keep.shape[0] // up_keep.shape[0]
    factor = HALF_ROOT * HALF_ROOT
    kept = spread(up_keep[...], times, factor)
    matrix = group_matrix(dk.shape[0], up_recv.shape[0], times, 1)
    received = dot(matrix, up_recv[...], NN) * factor
    mine = pl.ds(pl.multiple_of(meta[0] * width, width), width)
    theirs = pl.ds(pl.multiple_of((1 - meta[0]) * width, width), width)
    dk[:, mine] = (dk_keep[...] + kept[:, :width]).astype(BF16)
    dv[:, mine] = (dv_keep[...] + kept[:, width:]).astype(BF16)
    dk[:, theirs] = (dk_recv[...].astype(F32) + received[:, :width]).astype(BF16)
    dv[:, theirs] = (dv_recv[...].astype(F32) + received[:, width:]).astype(BF16)


def place_body(meta, keep, received, out):
    @pl.when(pl.program_id(0) == 0)
    def _():
        out[...] = keep[...]

    @pl.when(pl.program_id(0) == 1)
    def _():
        out[...] = received[...]


def place_halves(meta, keep, received):
    rows, cols = keep.shape
    return call(
        place_body,
        meta,
        (keep, received),
        [whole(keep), whole(received)],
        struct(rows, 2 * cols, keep.dtype),
        pl.BlockSpec((rows, cols), lambda i, m: (0, (m[0] + i) % 2)),
        grid=(2,),
    )


def other_half(array, bit):
    width = array.shape[1] // 2
    return lax.dynamic_slice_in_dim(array, (1 - bit) * width, width, 1)


def body(queries, keys, values, out_weight, out_grad):
    inner = queries.shape[2]
    half = inner // 2
    length = queries.shape[1]
    heads = HEADS // 2
    seq_count = lax.axis_size("seq")
    seq_levels = seq_count.bit_length() - 1
    dp_count = lax.axis_size("dp")
    rank = lax.axis_index("seq")
    bit = rank % 2
    pair = rank // 2
    token_total = length * seq_count * queries.shape[0] * dp_count

    up = [1 << level for level in reversed(range(1, seq_levels))]
    orders = (up, up[:-2] + up[:-3:-1])
    stages = list(zip(*orders, strict=True))
    pieces = seq_count // 2
    masks = [
        [sum(m for s, m in enumerate(order) if index >> s & 1) // 2 for index in range(pieces)]
        for order in orders
    ]
    table = pair ^ jnp.where(bit == 0, jnp.array(masks[0]), jnp.array(masks[1]))
    meta = jnp.concatenate([jnp.reshape(bit, (1,)), table]).astype(jnp.int32)

    query = queries[0]
    key = keys[0]
    value = values[0]
    grad = out_grad[0]
    if dp_count > 1:
        out_weight = lax.all_gather(out_weight, "dp", axis=1, tiled=True)
    cols = out_weight.shape[1] // 2
    piece = 2 * out_weight.shape[0]

    kv_other = swap(jnp.concatenate([other_half(key, bit), other_half(value, bit)], axis=1), 1)
    w_mine = lax.dynamic_slice_in_dim(out_weight, bit * cols, cols, 1)
    w_theirs = swap(other_half(out_weight, bit), 1)
    q_other = swap(other_half(query, bit), 1)
    g_other = swap(other_half(grad, bit), 1)

    sizes = [length // 2, length // 2] + [2 * length >> level for level in range(2, seq_levels + 1)]
    shapes = [struct(rows, inner, BF16) for rows in sizes]
    pooled = call(
        pool_body,
        meta,
        (key, value, kv_other),
        [own_half(key), own_half(value), whole(kv_other)],
        shapes,
        [whole(s) for s in shapes],
    )
    next_own, next_other = pooled[:2]
    coarse = dict(zip(range(1, seq_levels), pooled[2:], strict=True))

    w_rows = jnp.where(
        bit == 0,
        jnp.concatenate([w_mine, w_theirs], axis=0),
        jnp.concatenate([w_theirs, w_mine], axis=0),
    )

    far_masks = [(h, (1 << h) + (low << 3)) for h in range(3, seq_levels) for low in range(1 << (h - 3))]
    high_parts = [swap(coarse[h], mask) for h, mask in far_masks]
    panels = [swap(coarse[1], 2), swap(coarse[2], 4), swap(coarse[2], 6)]
    high = jnp.concatenate(high_parts, axis=0)
    panels += [high, swap(high, 2), swap(high, 4), swap(high, 6)]
    n_far = len(panels)

    for step, stage in enumerate(stages):
        received = permute(w_rows, stage)
        if step + 1 < len(stages):
            w_rows = jnp.concatenate([w_rows, received], axis=0)
    w_first, w_second = w_rows, received

    per_step = 2
    steps = heads // per_step
    width = per_step * HS

    def of_own(array):
        return pl.BlockSpec((array.shape[0], width), lambda i, m: (0, m[0] * steps + i))

    def left(array):
        return pl.BlockSpec((array.shape[0], width), lambda i, m: (0, i))

    def right(array):
        return pl.BlockSpec((array.shape[0], width), lambda i, m: (0, steps + i))

    key_count = length + length // 2 + sum(p.shape[0] for p in panels)
    token_ops = (query, q_other, key, value, kv_other, kv_other)
    token_specs = [of_own(query), left(q_other), of_own(key), of_own(value), left(kv_other), right(kv_other)]
    panel_ops = (next_other, next_own, next_other, next_own, *panels, *panels)
    panel_specs = [left(next_other), left(next_own), right(next_other), right(next_own)]
    panel_specs += [left(p) for p in panels] + [right(p) for p in panels]
    probs_shape = jax.ShapeDtypeStruct((2 * heads, key_count, length), BF16)
    probs_spec = pl.BlockSpec((2 * per_step, key_count, length), lambda i, m: (i, 0, 0))
    one_matmul = 2 * 2 * length * key_count * half
    attn_mine, probs = call(
        lambda *refs: forward_body(per_step, n_far, *refs),
        meta,
        token_ops + panel_ops,
        token_specs + panel_specs,
        [struct(half, 2 * length, BF16), probs_shape],
        [pl.BlockSpec((width, 2 * length), lambda i, m: (i, 0)), probs_spec],
        grid=(steps,),
        flops=2 * one_matmul,
    )
    attn_theirs = swap(attn_mine, 1)

    half_rows = pieces * piece // 2
    scratch = [pltpu.VMEM((2 * half_rows, cols), BF16)]
    g_spec = [own_half(grad), whole(g_other)]
    half_shape = struct(half_rows, cols, BF16)
    proj_flops = 2 * 2 * length * inner * cols
    wg_keep, wg_send = call(
        lambda *refs: weight_grad_body(piece, *refs),
        meta,
        (attn_mine, attn_theirs, grad, g_other),
        [whole(attn_mine), whole(attn_theirs)] + g_spec,
        [half_shape, half_shape],
        [whole(half_shape), whole(half_shape)],
        scratch,
        flops=proj_flops,
    )
    for step, stage in enumerate(reversed(stages)):
        received = permute(wg_send, stage)
        total = wg_keep.astype(F32) + received.astype(F32)
        if step + 1 < len(stages):
            total = total.astype(BF16)
            rows = total.shape[0] // 2
            wg_keep, wg_send = total[:rows], total[rows:]
    rows = piece // 2
    wg_mine = lax.dynamic_slice_in_dim(total, bit * rows, rows, 0)
    wg_theirs = swap(lax.dynamic_slice_in_dim(total, (1 - bit) * rows, rows, 0).astype(BF16), 1)
    wg_theirs = wg_theirs.astype(F32)
    weight_grad = jnp.where(
        bit == 0,
        jnp.concatenate([wg_mine, wg_theirs], axis=1),
        jnp.concatenate([wg_theirs, wg_mine], axis=1),
    )
    if dp_count > 1:
        weight_grad = lax.psum_scatter(
            weight_grad.astype(BF16), "dp", scatter_dimension=1, tiled=True
        ).astype(F32)
    weight_grad = weight_grad * (1.0 / math.sqrt(token_total))

    w_spec = [whole(w_first), whole(w_second)]
    d_shapes = [struct(2 * length, half, F32), struct(2 * length, half, BF16)]
    d_keep, d_send = call(
        lambda *refs: d_attn_body(piece, *refs),
        meta,
        (grad, g_other, w_first, w_second),
        g_spec + w_spec,
        d_shapes,
        [whole(s) for s in d_shapes],
        scratch,
        flops=proj_flops,
    )
    d_recv = swap(d_send, 1)

    out_shapes = [struct(length, half, BF16)] * 2
    out_shapes += [struct(length, half, F32), struct(length, half, BF16)] * 2
    out_shapes += [struct(p.shape[0], half, BF16) for p in panels] * 2
    grads = call(
        lambda *refs: backward_body(per_step, n_far, *refs),
        meta,
        token_ops + (d_keep, d_recv, probs) + panel_ops,
        token_specs + [left(d_keep), left(d_recv), probs_spec] + panel_specs,
        out_shapes,
        [left(s) for s in out_shapes],
        grid=(steps,),
        flops=4 * one_matmul,
    )
    dq_keep, dq_send, dk_keep, dk_send, dv_keep, dv_send = grads[:6]
    panel_grads = [
        jnp.concatenate([dk, dv], axis=1)
        for dk, dv in zip(grads[6 : 6 + n_far], grads[6 + n_far :], strict=True)
    ]

    high_sum = panel_grads[3].astype(F32)
    for part, mask in zip(panel_grads[4:], (2, 4, 6), strict=True):
        high_sum = high_sum + swap(part, mask).astype(F32)
    high_sum = high_sum.astype(BF16)
    by_level = {1: [swap(panel_grads[0], 2)], 2: [swap(panel_grads[1], 4), swap(panel_grads[2], 6)]}
    start = 0
    for h, mask in far_masks:
        rows = coarse[h].shape[0]
        by_level.setdefault(h, []).append(swap(high_sum[start : start + rows], mask))
        start += rows
    levels = list(reversed(range(1, seq_levels)))
    received = [part for h in levels for part in by_level[h]]
    counts = [len(by_level[h]) for h in levels]
    up_rows = coarse[1].shape[0] // 2
    up_shapes = [struct(up_rows, inner, F32), struct(up_rows, inner, BF16)]
    up_keep, up_send = call(
        lambda *refs: cascade_body(counts, *refs),
        meta,
        received,
        [whole(r) for r in received],
        up_shapes,
        [whole(s) for s in up_shapes],
    )
    up_recv = swap(up_send, 1)
    dk_recv = swap(dk_send, 1)
    dv_recv = swap(dv_send, 1)
    dq_recv = swap(dq_send, 1)
    fin_ops = (dk_keep, dv_keep, dk_recv, dv_recv, up_keep, up_recv)
    fin_shape = struct(length, inner, BF16)
    grad_keys, grad_values = call(
        finish_body,
        meta,
        fin_ops,
        [whole(o) for o in fin_ops],
        [fin_shape, fin_shape],
        [whole(fin_shape), whole(fin_shape)],
    )
    grad_queries = place_halves(meta, dq_keep, dq_recv)

    at_shape = struct(length, cols, BF16)
    at_keep, at_send = call(
        lambda *refs: attended_body(piece, *refs),
        meta,
        (attn_mine, attn_theirs, w_first, w_second),
        [whole(attn_mine), whole(attn_theirs)] + w_spec,
        [at_shape, at_shape],
        [whole(at_shape), whole(at_shape)],
        scratch,
        flops=proj_flops,
    )
    attended = place_halves(meta, at_keep, swap(at_send, 1))
    return (attended[None], grad_queries[None], grad_keys[None], grad_values[None], weight_grad)


def solution(mesh):
    placed = (
        P("dp", "seq", None),
        P("dp", "seq", None),
        P("dp", "seq", None),
        P("seq", "dp"),
        P("dp", "seq", None),
    )
    return jax.shard_map(
        body,
        mesh=mesh,
        in_specs=placed,
        out_specs=(
            P("dp", "seq", None),
            P("dp", "seq", None),
            P("dp", "seq", None),
            P("dp", "seq", None),
            P("seq", "dp"),
        ),
        check_vma=False,
    )
```

```python
import math

import jax
import jax.numpy as jnp
from jax import lax
from jax.experimental import pallas as pl
from jax.experimental.pallas import tpu as pltpu
from jax.sharding import PartitionSpec as P

HEADS = 8
HS = 128
NR = 128

HALF_ROOT = 0.7071067811865476
SCORE_SCALE = 1.0 / math.sqrt(HS)
EXP2_SCALE = SCORE_SCALE * math.log2(math.e)
F32 = jnp.float32
BF16 = jnp.bfloat16
VMEM_LIMIT = 40 * 1024 * 1024


def permute(value, masks):
    count = lax.axis_size("seq")
    return lax.ppermute(value, "seq", [(i, i ^ masks[i & 1]) for i in range(count)])


def swap(value, mask):
    return permute(value, (mask, mask))


def after(value, *others):
    return lax.optimization_barrier((value, *others))[0]


def call(body, meta, operands, specs, shapes, out_specs, scratch=(), grid=(1,)):
    return pl.pallas_call(
        body,
        grid_spec=pltpu.PrefetchScalarGridSpec(
            num_scalar_prefetch=1,
            grid=grid,
            in_specs=specs,
            out_specs=out_specs,
            scratch_shapes=list(scratch),
        ),
        out_shape=shapes,
        compiler_params=pltpu.CompilerParams(vmem_limit_bytes=VMEM_LIMIT),
        cost_estimate=pl.CostEstimate(flops=0, bytes_accessed=0, transcendentals=0),
    )(meta, *operands)


def whole(array):
    return pl.BlockSpec(array.shape, lambda i, m: (0,) * len(array.shape))


def own_half(array):
    return pl.BlockSpec((array.shape[0], array.shape[1] // 2), lambda i, m: (0, m[0]))


def struct(rows, cols, dtype):
    return jax.ShapeDtypeStruct((rows, cols), dtype)


def planes(rows, cols, dtype):
    return jax.ShapeDtypeStruct((2, rows, cols), dtype)


def dot(a, b, dims):
    return lax.dot_general(a, b, (dims, ((), ())), preferred_element_type=F32)


NN = ((1,), (0,))
NT = ((1,), (1,))
TN = ((0,), (0,))


def group_matrix(rows, cols, row_div, col_div):
    row = lax.broadcasted_iota(jnp.int32, (rows, cols), 0) // row_div
    col = lax.broadcasted_iota(jnp.int32, (rows, cols), 1) // col_div
    return jnp.where(row == col, 1.0, 0.0).astype(BF16)


def pool(rows):
    half = rows.shape[0] // 2
    return (dot(group_matrix(half, 2 * half, 1, 2), rows, NN) * HALF_ROOT).astype(BF16)


def spread(grad, times, factor):
    high = grad.astype(BF16)
    low = (grad - high.astype(F32)).astype(BF16)
    matrix = group_matrix(times * grad.shape[0], grad.shape[0], times, 1)
    return (dot(matrix, high, NN) + dot(matrix, low, NN)) * factor


def lanes(ref):
    return jnp.concatenate([ref[0], ref[1]], axis=1)


def put_planes(ref, rows):
    width = ref.shape[2]
    ref[0] = rows[:, :width].astype(ref.dtype)
    ref[1] = rows[:, width:].astype(ref.dtype)


def pool_body(meta, keys, values, other, *outs):
    own = jnp.concatenate([keys[...], values[...]], axis=1)
    first_own = pool(own)
    first_other = pool(lanes(other))
    put_planes(outs[0], first_own)
    put_planes(outs[1], first_other)
    rows = jnp.concatenate([pool(first_own), pool(first_other)], axis=0)
    put_planes(outs[2], rows)
    for out in outs[3:]:
        rows = pool(rows)
        put_planes(out, rows)


def key_sets(k_own, v_own, kv_other, next_own, next_other, far, at):
    far_rows = [[ref[plane, start : start + rows, at] for ref, start, rows in far] for plane in range(2)]
    near = ((k_own[:, at], kv_other[0, :, at]), (v_own[:, at], kv_other[1, :, at]))
    coarse = (next_other, next_own)
    return [
        [
            jnp.concatenate([near[plane][group], coarse[group][plane, :, at]] + far_rows[plane], axis=0)
            for group in range(2)
        ]
        for plane in range(2)
    ]


def forward_body(heads, parts, meta, q_own, q_other, k_own, v_own, kv_other, next_own, next_other, *refs):
    n_far = len(refs) - 2
    attn_ref, probs_ref = refs[n_far:]
    far = [(refs[index], start, rows) for index, start, rows in parts]
    for head in range(heads):
        at = slice(head * HS, (head + 1) * HS)
        keys, values = key_sets(k_own, v_own, kv_other, next_own, next_other, far, at)
        for group, q_ref in enumerate((q_own, q_other)):
            length = q_ref.shape[0]
            scores = dot(keys[group], q_ref[:, at], NT)
            top = jnp.max(scores, axis=0, keepdims=True)
            weights = jnp.exp2((scores - top) * EXP2_SCALE)
            total = jnp.sum(weights, axis=0, keepdims=True)
            probs = (weights * (1.0 / total)).astype(BF16)
            probs_ref[2 * head + group] = probs
            attn = dot(values[group], probs, TN)
            attn_ref[at, group * length : (group + 1) * length] = attn.astype(BF16)


def backward_body(
    heads, parts, n_far, meta, q_own, q_other, k_own, v_own, kv_other, next_own, next_other, *refs
):
    far = [(refs[index], start, rows) for index, start, rows in parts]
    d_keep, d_recv, probs_ref, dq_own, dq_other, near_own, near_other = refs[n_far : n_far + 7]
    far_grads = refs[n_far + 7 :]
    near_rows = k_own.shape[0]
    after_next = near_rows + next_own.shape[1]
    for head in range(heads):
        at = slice(head * HS, (head + 1) * HS)
        keys, values = key_sets(k_own, v_own, kv_other, next_own, next_other, far, at)
        grads = ([], [])
        for group, (q_ref, dq_ref) in enumerate(((q_own, dq_own), (q_other, dq_other))):
            length = q_ref.shape[0]
            rows = slice(group * length, (group + 1) * length)
            d_attn = (d_keep[rows, at] + d_recv[rows, at].astype(F32)).astype(BF16)
            probs_low = probs_ref[2 * head + group]
            probs = probs_low.astype(F32)
            d_prob = dot(values[group], d_attn, NT)
            center = jnp.sum(probs * d_prob, axis=0, keepdims=True)
            d_score = (probs * (d_prob - center)).astype(BF16)
            dq = dot(keys[group], d_score, TN) * SCORE_SCALE
            dq_ref[:, at] = dq.T.astype(BF16)
            grads[0].append(dot(d_score, q_ref[:, at], NN) * SCORE_SCALE)
            grads[1].append(dot(probs_low, d_attn, NN))
        for plane in range(2):
            for group, near in enumerate((near_own, near_other)):
                total = grads[plane][group][:near_rows]
                total = total + spread(grads[plane][1 - group][near_rows:after_next], 2, HALF_ROOT)
                near[plane, :, at] = total.astype(near.dtype)
            total = grads[plane][0][after_next:] + grads[plane][1][after_next:]
            done = 0
            for index, start, rows in parts:
                out = far_grads[index]
                out[plane, start : start + rows, at] = total[done : done + rows].astype(BF16)
                done += rows


def pieces_of(quarters, piece):
    return [(quarter, start) for quarter in quarters for start in range(0, quarter.shape[0], piece)]


def rows_of_piece(meta, masks, index, piece):
    owner = meta[1] ^ jnp.where(meta[0] == 0, masks[0][index], masks[1][index])
    return pl.ds(pl.multiple_of(owner * piece, piece), piece)


def ordered_weight(meta, quarters, scratch, piece, masks):
    for index, (quarter, start) in enumerate(pieces_of(quarters, piece)):
        scratch[rows_of_piece(meta, masks, index, piece), :] = quarter[start : start + piece, :]


def half_rows_of(meta, scratch, mine):
    width = scratch.shape[0] // 2
    start = meta[0] * width if mine else (1 - meta[0]) * width
    return pl.ds(pl.multiple_of(start, width), width)


def d_attn_body(piece, masks, meta, grad_own, grad_other, *refs):
    keep, send, scratch = refs[-3:]
    ordered_weight(meta, refs[:-3], scratch, piece, masks)
    length = grad_own.shape[0]
    mine = scratch[half_rows_of(meta, scratch, True), :]
    theirs = scratch[half_rows_of(meta, scratch, False), :]
    send[:length] = dot(grad_other[...], theirs, NT).astype(BF16)
    send[length:] = dot(grad_own[...], theirs, NT).astype(BF16)
    keep[:length] = dot(grad_own[...], mine, NT)
    keep[length:] = dot(grad_other[...], mine, NT)


def attended_body(piece, masks, meta, attn_mine, attn_theirs, *refs):
    keep, send, scratch = refs[-3:]
    ordered_weight(meta, refs[:-3], scratch, piece, masks)
    length = keep.shape[0]
    mine = scratch[half_rows_of(meta, scratch, True), :]
    theirs = scratch[half_rows_of(meta, scratch, False), :]
    send[...] = (
        dot(attn_mine[:, length:], mine, TN) + dot(attn_theirs[:, :length], theirs, TN)
    ).astype(BF16)
    keep[...] = (
        dot(attn_mine[:, :length], mine, TN) + dot(attn_theirs[:, length:], theirs, TN)
    ).astype(BF16)


def weight_grad_body(piece, masks, meta, attn_mine, attn_theirs, grad_own, grad_other, *refs):
    scratch = refs[-1]
    length = grad_own.shape[0]
    mine = dot(attn_mine[:, :length], grad_own[...], NN) + dot(
        attn_mine[:, length:], grad_other[...], NN
    )
    scratch[half_rows_of(meta, scratch, True), :] = mine.astype(BF16)
    theirs = dot(attn_theirs[:, length:], grad_own[...], NN) + dot(
        attn_theirs[:, :length], grad_other[...], NN
    )
    scratch[half_rows_of(meta, scratch, False), :] = theirs.astype(BF16)
    for index, (quarter, start) in enumerate(pieces_of(refs[:-1], piece)):
        quarter[start : start + piece, :] = scratch[rows_of_piece(meta, masks, index, piece), :]


def high_body(cuts, skips, meta, own, *refs):
    received = refs[: len(skips)]
    for plane in range(2):
        total = own[plane].astype(F32)
        for ref, skip in zip(received, skips, strict=True):
            total = total + ref[plane, skip:].astype(F32)
        start = 0
        for out, rows in zip(refs[len(skips) :], cuts, strict=True):
            out[plane] = total[start : start + rows].astype(BF16)
            start += rows


def cascade_body(counts, meta, *refs):
    keep, send = refs[-2:]
    half = keep.shape[1]
    total = None
    start = 0
    rows = 2 * half >> (len(counts) - 1)
    for count in counts:
        level = lanes(refs[start])[:rows].astype(F32)
        for ref in refs[start + 1 : start + count]:
            level = level + lanes(ref)[:rows].astype(F32)
        start += count
        rows *= 2
        total = level if total is None else level + spread(total, 2, HALF_ROOT)
    put_planes(keep, total[:half])
    put_planes(send, total[half:])


def finish_body(meta, near_keep, near_recv, up_keep, up_recv, dk, dv):
    width = near_keep.shape[2]
    times = near_keep.shape[1] // up_keep.shape[1]
    factor = HALF_ROOT * HALF_ROOT
    matrix = group_matrix(dk.shape[0], up_recv.shape[1], times, 1)
    mine = pl.ds(pl.multiple_of(meta[0] * width, width), width)
    theirs = pl.ds(pl.multiple_of((1 - meta[0]) * width, width), width)
    for plane, out in enumerate((dk, dv)):
        out[:, mine] = (near_keep[plane] + spread(up_keep[plane], times, factor)).astype(BF16)
        received = dot(matrix, up_recv[plane], NN) * factor
        out[:, theirs] = (near_recv[plane].astype(F32) + received).astype(BF16)


def place_body(meta, keep, received, out):
    @pl.when(pl.program_id(0) == 0)
    def _():
        out[...] = keep[...]

    @pl.when(pl.program_id(0) == 1)
    def _():
        out[...] = received[...]


def place_halves(meta, keep, received):
    rows, cols = keep.shape
    return call(
        place_body,
        meta,
        (keep, received),
        [whole(keep), whole(received)],
        struct(rows, 2 * cols, keep.dtype),
        pl.BlockSpec((rows, cols), lambda i, m: (0, (m[0] + i) % 2)),
        grid=(2,),
    )


def other_half(array, bit):
    width = array.shape[1] // 2
    return lax.dynamic_slice_in_dim(array, (1 - bit) * width, width, 1)


def body(queries, keys, values, out_weight, out_grad):
    inner = queries.shape[2]
    half = inner // 2
    length = queries.shape[1]
    heads = HEADS // 2
    seq_count = lax.axis_size("seq")
    seq_levels = seq_count.bit_length() - 1
    dp_count = lax.axis_size("dp")
    rank = lax.axis_index("seq")
    bit = rank % 2
    pair = rank // 2
    token_total = length * seq_count * queries.shape[0] * dp_count

    up = [1 << level for level in reversed(range(1, seq_levels))]
    orders = (up[:-2] + [2, 4], [2] + up[:-3] + [4, 8])
    stages = list(zip(*orders, strict=True))
    pieces = seq_count // 2
    masks = [
        [sum(m for s, m in enumerate(order) if index >> s & 1) // 2 for index in range(pieces)]
        for order in orders
    ]
    meta = jnp.stack([bit, pair]).astype(jnp.int32)

    query = queries[0]
    key = keys[0]
    value = values[0]
    grad = out_grad[0]
    if dp_count > 1:
        out_weight = lax.all_gather(out_weight, "dp", axis=1, tiled=True)
    cols = out_weight.shape[1] // 2
    piece = 2 * out_weight.shape[0]

    kv_other = swap(jnp.stack([other_half(key, bit), other_half(value, bit)]), 1)
    w_mine = lax.dynamic_slice_in_dim(out_weight, bit * cols, cols, 1)
    w_theirs = swap(other_half(out_weight, bit), 1)

    sizes = [length // 2, length // 2] + [2 * length >> level for level in range(2, seq_levels + 1)]
    shapes = [planes(rows, half, BF16) for rows in sizes]
    pooled = call(
        pool_body,
        meta,
        (key, value, kv_other),
        [own_half(key), own_half(value), whole(kv_other)],
        shapes,
        [whole(s) for s in shapes],
    )
    next_own, next_other = pooled[:2]
    coarse = dict(zip(range(1, seq_levels), pooled[2:], strict=True))

    w_rows = jnp.where(
        bit == 0,
        jnp.concatenate([w_mine, w_theirs], axis=0),
        jnp.concatenate([w_theirs, w_mine], axis=0),
    )
    w_received = permute(w_rows, stages[0])
    far_masks = [(h, (1 << h) + (low << 3)) for h in range(3, seq_levels) for low in range(1 << (h - 3))]
    high_parts = [swap(coarse[h], mask) for h, mask in far_masks]
    first_panel = swap(coarse[1], 2)
    w_received, *high_parts = lax.optimization_barrier((w_received, *high_parts))

    high = jnp.concatenate(high_parts, axis=1)
    second = jnp.concatenate([coarse[2], high], axis=1)
    panels = [high, first_panel, swap(high, 2), swap(second, 4), swap(second, 6)]
    for stage in stages[1:-2]:
        w_rows = jnp.concatenate([w_rows, w_received], axis=0)
        w_received = permute(w_rows, stage)
    q_other = swap(after(other_half(query, bit), high), 1)
    g_other = swap(after(other_half(grad, bit), high), 1)
    n_high, n_second = high.shape[1], coarse[2].shape[1]
    parts = ((1, 0, coarse[1].shape[1]), (3, 0, n_second), (4, 0, n_second))
    parts += ((0, 0, n_high), (2, 0, n_high), (3, n_second, n_high), (4, n_second, n_high))

    w_rows = jnp.concatenate([w_rows, after(w_received, *panels)], axis=0)
    w_received = permute(w_rows, stages[-2])
    w_last = permute(w_rows, stages[-1])

    per_step = 2
    steps = heads // per_step
    width = per_step * HS

    def of_own(array):
        return pl.BlockSpec((array.shape[0], width), lambda i, m: (0, m[0] * steps + i))

    def left(array):
        return pl.BlockSpec((array.shape[0], width), lambda i, m: (0, i))

    def both(array):
        return pl.BlockSpec((2, array.shape[1], width), lambda i, m: (0, 0, i))

    key_count = length + length // 2 + sum(rows for _, _, rows in parts)
    plane_ops = (kv_other, next_own, next_other, *panels)
    att_ops = (query, q_other, key, value, *plane_ops)
    att_specs = [of_own(query), left(q_other), of_own(key), of_own(value)] + [both(a) for a in plane_ops]
    probs_shape = jax.ShapeDtypeStruct((2 * heads, key_count, length), BF16)
    probs_spec = pl.BlockSpec((2 * per_step, key_count, length), lambda i, m: (i, 0, 0))
    attn_mine, probs = call(
        lambda *refs: forward_body(per_step, parts, *refs),
        after(meta, w_rows),
        att_ops,
        att_specs,
        [struct(half, 2 * length, BF16), probs_shape],
        [pl.BlockSpec((width, 2 * length), lambda i, m: (i, 0)), probs_spec],
        grid=(steps,),
    )

    w_received = after(w_received, attn_mine)
    quarters = (w_rows, w_received, w_last, permute(w_received, stages[-1]))
    attn_theirs = swap(attn_mine, 1)

    scratch = [pltpu.VMEM((pieces * piece, cols), BF16)]
    g_spec = [own_half(grad), whole(g_other)]
    wg_shapes = [struct(pieces * piece // 4, cols, BF16)] * 4
    wg = call(
        lambda *refs: weight_grad_body(piece, masks, *refs),
        meta,
        (attn_mine, attn_theirs, grad, g_other),
        [whole(attn_mine), whole(attn_theirs)] + g_spec,
        wg_shapes,
        [whole(s) for s in wg_shapes],
        scratch,
    )
    wg_received = [permute(after(part, quarters[3]), stages[-1]) for part in (wg[3], wg[2])]

    w_spec = [whole(quarter) for quarter in quarters]
    d_shapes = [struct(2 * length, half, F32), struct(2 * length, half, BF16)]
    d_keep, d_send = call(
        lambda *refs: d_attn_body(piece, masks, *refs),
        after(meta, wg[0]),
        (grad, g_other, *quarters),
        g_spec + w_spec,
        d_shapes,
        [whole(s) for s in d_shapes],
        scratch,
    )
    d_recv = swap(d_send, 1)

    out_shapes = [struct(length, half, BF16)] * 2
    out_specs = [left(s) for s in out_shapes]
    plane_shapes = [planes(length, half, F32), planes(length, half, BF16)]
    plane_shapes += [planes(p.shape[1], half, BF16) for p in panels[:1]]
    plane_shapes += [planes(p.shape[1], half, BF16) for p in panels[1:]]
    grads = call(
        lambda *refs: backward_body(per_step, parts, len(panels), *refs),
        meta,
        att_ops + (d_keep, d_recv, probs),
        att_specs + [left(d_keep), left(d_recv), probs_spec],
        out_shapes + plane_shapes,
        out_specs + [both(s) for s in plane_shapes],
        grid=(steps,),
    )
    dq_keep, dq_send, near_keep, near_send, high_own, first_grad, *rest = grads

    def add(kept, received):
        return (kept.astype(F32) + received.astype(F32)).astype(BF16)

    wg_send = add(wg[1], after(wg_received[0], dq_keep))
    wg_keep = add(wg[0], after(wg_received[1], dq_keep))
    wg_received = permute(wg_send, stages[-2])

    first_back = swap(first_grad, 2)
    back = [swap(part, mask) for part, mask in zip(rest, (2, 4, 6), strict=True)]
    cuts = [coarse[h].shape[1] for h, _ in far_masks]
    high_shapes = [planes(rows, half, BF16) for rows in cuts]
    high_sums = call(
        lambda *refs: high_body(cuts, (0, n_second, n_second), *refs),
        meta,
        (high_own, *back),
        [whole(high_own)] + [whole(b) for b in back],
        high_shapes,
        [whole(s) for s in high_shapes],
    )
    by_level = {1: [first_back], 2: back[1:]}
    for (h, mask), part in zip(far_masks, high_sums, strict=True):
        by_level.setdefault(h, []).append(swap(part, mask))
    near_recv = swap(after(near_send, first_grad), 1)
    dq_recv = swap(after(dq_send, first_grad), 1)
    grad_queries = place_halves(meta, dq_keep, dq_recv)

    at_shape = struct(length, cols, BF16)
    at_keep, at_send = call(
        lambda *refs: attended_body(piece, masks, *refs),
        after(meta, first_grad),
        (attn_mine, attn_theirs, *quarters),
        [whole(attn_mine), whole(attn_theirs)] + w_spec,
        [at_shape, at_shape],
        [whole(at_shape), whole(at_shape)],
        scratch,
    )
    attended = place_halves(meta, at_keep, swap(at_send, 1))

    for stage in reversed(stages[:-2]):
        total = add(wg_keep, wg_received)
        rows = total.shape[0] // 2
        wg_keep, wg_send = total[:rows], total[rows:]
        wg_received = permute(wg_send, stage)
    total = wg_keep.astype(F32) + wg_received.astype(F32)
    rows = piece // 2
    wg_mine = lax.dynamic_slice_in_dim(total, bit * rows, rows, 0)
    wg_theirs = swap(lax.dynamic_slice_in_dim(total, (1 - bit) * rows, rows, 0).astype(BF16), 1)
    wg_theirs = wg_theirs.astype(F32)
    weight_grad = jnp.where(
        bit == 0,
        jnp.concatenate([wg_mine, wg_theirs], axis=1),
        jnp.concatenate([wg_theirs, wg_mine], axis=1),
    )
    if dp_count > 1:
        weight_grad = lax.psum_scatter(
            weight_grad.astype(BF16), "dp", scatter_dimension=1, tiled=True
        ).astype(F32)
    weight_grad = weight_grad * (1.0 / math.sqrt(token_total))

    levels = list(reversed(range(1, seq_levels)))
    received = [part for h in levels for part in by_level[h]]
    counts = [len(by_level[h]) for h in levels]
    up_rows = coarse[1].shape[1] // 2
    up_shapes = [planes(up_rows, half, F32), planes(up_rows, half, BF16)]
    up_keep, up_send = call(
        lambda *refs: cascade_body(counts, *refs),
        meta,
        received,
        [whole(r) for r in received],
        up_shapes,
        [whole(s) for s in up_shapes],
    )
    fin_ops = (near_keep, near_recv, up_keep, swap(up_send, 1))
    fin_shape = struct(length, inner, BF16)
    grad_keys, grad_values = call(
        finish_body,
        meta,
        fin_ops,
        [whole(o) for o in fin_ops],
        [fin_shape, fin_shape],
        [whole(fin_shape), whole(fin_shape)],
    )
    return (attended[None], grad_queries[None], grad_keys[None], grad_values[None], weight_grad)


def solution(mesh):
    placed = (
        P("dp", "seq", None),
        P("dp", "seq", None),
        P("dp", "seq", None),
        P("seq", "dp"),
        P("dp", "seq", None),
    )
    return jax.shard_map(
        body,
        mesh=mesh,
        in_specs=placed,
        out_specs=(
            P("dp", "seq", None),
            P("dp", "seq", None),
            P("dp", "seq", None),
            P("dp", "seq", None),
            P("seq", "dp"),
        ),
        check_vma=False,
    )
```

```python
import math

import jax
import jax.numpy as jnp
from jax import lax
from jax.experimental import pallas as pl
from jax.experimental.pallas import tpu as pltpu
from jax.sharding import PartitionSpec as P

HEADS = 8
HS = 128
NR = 128

HALF_ROOT = 0.7071067811865476
SCORE_SCALE = 1.0 / math.sqrt(HS)
EXP2_SCALE = SCORE_SCALE * math.log2(math.e)
F32 = jnp.float32
BF16 = jnp.bfloat16
VMEM_LIMIT = 20 * 1024 * 1024


def permute(value, masks):
    count = lax.axis_size("seq")
    return lax.ppermute(value, "seq", [(i, i ^ masks[i & 1]) for i in range(count)])


def swap(value, mask):
    return permute(value, (mask, mask))


def after(value, *others):
    return lax.optimization_barrier((value, *others))[0]


def call(body, meta, operands, shapes, scratch=(), last=False, flops=0):
    specs = [pl.BlockSpec(memory_space=pltpu.VMEM) for _ in operands]
    if last:
        out_specs = [pl.BlockSpec(s.shape, lambda i: (0,) * len(s.shape)) for s in shapes]
    else:
        out_specs = [pl.BlockSpec(memory_space=pltpu.VMEM) for _ in shapes]
    return pl.pallas_call(
        body,
        grid=(1,) if last else (),
        in_specs=[pl.BlockSpec(memory_space=pltpu.SMEM)] + specs,
        out_specs=out_specs,
        out_shape=shapes,
        scratch_shapes=list(scratch),
        compiler_params=pltpu.CompilerParams(vmem_limit_bytes=VMEM_LIMIT),
        cost_estimate=pl.CostEstimate(flops=flops, bytes_accessed=0, transcendentals=0),
    )(meta, *operands)


def struct(rows, cols, dtype):
    return jax.ShapeDtypeStruct((rows, cols), dtype)


def planes(rows, cols, dtype):
    return jax.ShapeDtypeStruct((2, rows, cols), dtype)


def dot(a, b, dims):
    return lax.dot_general(a, b, (dims, ((), ())), preferred_element_type=F32)


NN = ((1,), (0,))
NT = ((1,), (1,))
TN = ((0,), (0,))


def group_matrix(rows, cols, row_div, col_div):
    row = lax.broadcasted_iota(jnp.int32, (rows, cols), 0) // row_div
    col = lax.broadcasted_iota(jnp.int32, (rows, cols), 1) // col_div
    return jnp.where(row == col, 1.0, 0.0).astype(BF16)


def pool(rows):
    half = rows.shape[0] // 2
    return (dot(group_matrix(half, 2 * half, 1, 2), rows, NN) * HALF_ROOT).astype(BF16)


def spread(grad, times, factor):
    high = grad.astype(BF16)
    low = (grad - high.astype(F32)).astype(BF16)
    matrix = group_matrix(times * grad.shape[0], grad.shape[0], times, 1)
    return (dot(matrix, high, NN) + dot(matrix, low, NN)) * factor


def lanes(ref):
    return jnp.concatenate([ref[0], ref[1]], axis=1)


def put_planes(ref, rows):
    width = ref.shape[2]
    ref[0] = rows[:, :width].astype(ref.dtype)
    ref[1] = rows[:, width:].astype(ref.dtype)


def half_of(meta, width, mine):
    start = meta[0] * width if mine else (1 - meta[0]) * width
    return pl.ds(pl.multiple_of(start, width), width)


def pool_body(meta, own, other, *outs):
    first_own = pool(lanes(own))
    first_other = pool(lanes(other))
    put_planes(outs[0], first_own)
    put_planes(outs[1], first_other)
    rows = jnp.concatenate([pool(first_own), pool(first_other)], axis=0)
    put_planes(outs[2], rows)
    for out in outs[3:]:
        rows = pool(rows)
        put_planes(out, rows)


def key_sets(kv_own, kv_other, next_own, next_other, far, at):
    near = (kv_own, kv_other)
    coarse = (next_other, next_own)
    sets = []
    for plane in range(2):
        far_rows = [ref[plane, start : start + rows, at] for ref, start, rows in far]
        sets.append(
            [
                jnp.concatenate([near[group][plane, :, at], coarse[group][plane, :, at]] + far_rows, axis=0)
                for group in range(2)
            ]
        )
    return sets


def forward_body(parts, meta, q_own, q_other, kv_own, kv_other, next_own, next_other, *refs):
    attn_ref, probs_ref = refs[-2:]
    far = [(refs[index], start, rows) for index, start, rows in parts]
    length, width = q_own.shape
    chunk = length // 2
    for head in range(width // HS):
        at = slice(head * HS, (head + 1) * HS)
        keys, values = key_sets(kv_own, kv_other, next_own, next_other, far, at)
        for group, q_ref in enumerate((q_own, q_other)):
            scores = dot(keys[group], q_ref[:, at], NT)
            for start in range(0, length, chunk):
                some = scores[:, start : start + chunk]
                top = jnp.max(some, axis=0, keepdims=True)
                weights = jnp.exp2((some - top) * EXP2_SCALE)
                total = jnp.sum(weights, axis=0, keepdims=True)
                probs = (weights * (1.0 / total)).astype(BF16)
                probs_ref[2 * head + group, :, start : start + chunk] = probs
                first = group * length + start
                attn_ref[first : first + chunk, at] = dot(probs, values[group], TN).astype(BF16)


def backward_body(
    parts, n_far, n_out, heads, meta, q_own, q_other, kv_own, kv_other, next_own, next_other, *refs
):
    far = [(refs[index], start, rows) for index, start, rows in parts]
    d_keep, d_recv, probs_ref = refs[n_far : n_far + 3]
    outs = refs[len(refs) - n_out :]
    for previous, out in zip(refs[n_far + 3 : len(refs) - n_out], outs, strict=False):
        out[..., : previous.shape[-1]] = previous[...]
    dq_own, dq_other, near_own, near_other, *far_grads = outs
    near_rows = kv_own.shape[1]
    after_next = near_rows + next_own.shape[1]
    for head in heads:
        at = slice(head * HS, (head + 1) * HS)
        keys, values = key_sets(kv_own, kv_other, next_own, next_other, far, at)
        grads = ([], [])
        for group, (q_ref, dq_ref) in enumerate(((q_own, dq_own), (q_other, dq_other))):
            length = q_ref.shape[0]
            rows = slice(group * length, (group + 1) * length)
            d_attn = (d_keep[rows, at] + d_recv[rows, at].astype(F32)).astype(BF16)
            probs_low = probs_ref[2 * head + group]
            probs = probs_low.astype(F32)
            d_prob = dot(values[group], d_attn, NT)
            center = jnp.sum(probs * d_prob, axis=0, keepdims=True)
            d_score = (probs * (d_prob - center)).astype(BF16)
            dq_ref[:, at] = (dot(d_score, keys[group], TN) * SCORE_SCALE).astype(BF16)
            grads[0].append(dot(d_score, q_ref[:, at], NN))
            grads[1].append(dot(probs_low, d_attn, NN))
        for plane, factor in enumerate((SCORE_SCALE, 1.0)):
            for group, near in enumerate((near_own, near_other)):
                mine, other = grads[plane][group], grads[plane][1 - group]
                near[plane, :near_rows, at] = (mine[:near_rows] * factor).astype(near.dtype)
                near[plane, near_rows:, at] = (other[near_rows:after_next] * factor).astype(near.dtype)
            total = (grads[plane][0][after_next:] + grads[plane][1][after_next:]) * factor
            done = 0
            for index, start, rows in parts:
                out = far_grads[index]
                out[plane, start : start + rows, at] = total[done : done + rows].astype(BF16)
                done += rows


def pieces_of(quarters, piece):
    return [(quarter, start) for quarter in quarters for start in range(0, quarter.shape[0], piece)]


def rows_of_piece(meta, masks, index, piece):
    owner = meta[1] ^ jnp.where(meta[0] == 0, masks[0][index], masks[1][index])
    return pl.ds(pl.multiple_of(owner * piece, piece), piece)


def ordered_weight(meta, quarters, scratch, piece, masks):
    for index, (quarter, start) in enumerate(pieces_of(quarters, piece)):
        scratch[rows_of_piece(meta, masks, index, piece), :] = quarter[start : start + piece, :]


def d_attn_body(piece, masks, meta, grad_own, grad_other, *refs):
    keep, send, scratch = refs[-3:]
    ordered_weight(meta, refs[:-3], scratch, piece, masks)
    length = grad_own.shape[0]
    mine = scratch[half_of(meta, keep.shape[1], True), :]
    theirs = scratch[half_of(meta, keep.shape[1], False), :]
    send[:length] = dot(grad_other[...], theirs, NT).astype(BF16)
    send[length:] = dot(grad_own[...], theirs, NT).astype(BF16)
    keep[:length] = dot(grad_own[...], mine, NT)
    keep[length:] = dot(grad_other[...], mine, NT)


def attended_body(piece, masks, meta, attn_mine, attn_theirs, *refs):
    keep, send, scratch = refs[-3:]
    ordered_weight(meta, refs[:-3], scratch, piece, masks)
    length = keep.shape[0]
    mine = scratch[half_of(meta, attn_mine.shape[1], True), :]
    theirs = scratch[half_of(meta, attn_mine.shape[1], False), :]
    send[...] = (
        dot(attn_mine[length:], mine, NN) + dot(attn_theirs[:length], theirs, NN)
    ).astype(BF16)
    keep[...] = (
        dot(attn_mine[:length], mine, NN) + dot(attn_theirs[length:], theirs, NN)
    ).astype(BF16)


def weight_grad_body(piece, masks, meta, attn_mine, attn_theirs, grad_own, grad_other, *refs):
    scratch = refs[-1]
    length = grad_own.shape[0]
    width = attn_mine.shape[1]
    mine = dot(attn_mine[:length], grad_own[...], TN) + dot(attn_mine[length:], grad_other[...], TN)
    scratch[half_of(meta, width, True), :] = mine.astype(BF16)
    theirs = dot(attn_theirs[length:], grad_own[...], TN) + dot(
        attn_theirs[:length], grad_other[...], TN
    )
    scratch[half_of(meta, width, False), :] = theirs.astype(BF16)
    for index, (quarter, start) in enumerate(pieces_of(refs[:-1], piece)):
        quarter[start : start + piece, :] = scratch[rows_of_piece(meta, masks, index, piece), :]


def high_body(cuts, skips, meta, own, *refs):
    received = refs[: len(skips)]
    for plane in range(2):
        total = own[plane].astype(F32)
        for ref, skip in zip(received, skips, strict=True):
            total = total + ref[plane, skip:].astype(F32)
        start = 0
        for out, rows in zip(refs[len(skips) :], cuts, strict=True):
            out[plane] = total[start : start + rows].astype(BF16)
            start += rows


def cascade_body(counts, meta, *refs):
    keep, send = refs[-2:]
    half = keep.shape[1]
    total = None
    start = 0
    rows = 2 * half >> (len(counts) - 1)
    for count in counts:
        level = lanes(refs[start])[:rows].astype(F32)
        for ref in refs[start + 1 : start + count]:
            level = level + lanes(ref)[:rows].astype(F32)
        start += count
        rows *= 2
        total = level if total is None else level + spread(total, 2, HALF_ROOT)
    put_planes(keep, total[:half])
    put_planes(send, total[half:])


def near_body(meta, keep, recv, dk, dv):
    rows, width = dk.shape[0], keep.shape[2]
    matrix = group_matrix(rows, keep.shape[1] - rows, 2, 1)
    for plane, out in enumerate((dk, dv)):
        own = keep[plane, :rows] + spread(keep[plane, rows:], 2, HALF_ROOT)
        out[:, half_of(meta, width, True)] = own
        other = recv[plane, :rows].astype(F32) + dot(matrix, recv[plane, rows:], NN) * HALF_ROOT
        out[:, half_of(meta, width, False)] = other


def finish_body(meta, base_k, base_v, up_keep, up_recv, dk, dv):
    rows, width = dk.shape[0], up_keep.shape[2]
    times = rows // up_keep.shape[1]
    factor = HALF_ROOT * HALF_ROOT
    matrix = group_matrix(rows, up_recv.shape[1], times, 1)
    mine, theirs = half_of(meta, width, True), half_of(meta, width, False)
    for plane, (base, out) in enumerate(((base_k, dk), (base_v, dv))):
        out[:, mine] = (base[:, mine] + spread(up_keep[plane], times, factor)).astype(BF16)
        received = dot(matrix, up_recv[plane], NN) * factor
        out[:, theirs] = (base[:, theirs] + received).astype(BF16)


def place_body(meta, *refs):
    outs = refs[2 * len(refs) // 3 :]
    for index, out in enumerate(outs):
        width = out.shape[1] // 2
        out[:, half_of(meta, width, True)] = refs[2 * index][...]
        out[:, half_of(meta, width, False)] = refs[2 * index + 1][...]


def body(queries, keys, values, out_weight, out_grad):
    inner = queries.shape[2]
    half = inner // 2
    length = queries.shape[1]
    heads = HEADS // 2
    seq_count = lax.axis_size("seq")
    seq_levels = seq_count.bit_length() - 1
    dp_count = lax.axis_size("dp")
    rank = lax.axis_index("seq")
    bit = rank % 2
    pair = rank // 2
    token_total = length * seq_count * queries.shape[0] * dp_count

    up = [1 << level for level in reversed(range(1, seq_levels))]
    orders = (up[:-2] + [2, 4], [2] + up[:-3] + [4, 8])
    stages = list(zip(*orders, strict=True))
    pieces = seq_count // 2
    masks = [
        [sum(m for s, m in enumerate(order) if index >> s & 1) // 2 for index in range(pieces)]
        for order in orders
    ]
    meta = jnp.stack([bit, pair]).astype(jnp.int32)

    query = queries[0]
    key = keys[0]
    value = values[0]
    grad = out_grad[0]
    if dp_count > 1:
        out_weight = lax.all_gather(out_weight, "dp", axis=1, tiled=True)
    cols = out_weight.shape[1] // 2
    piece = 2 * out_weight.shape[0]

    def part(array, which):
        width = array.shape[1] // 2
        return lax.dynamic_slice_in_dim(array, which * width, width, 1)

    q_half = struct(length, half, BF16)
    g_half = struct(length, cols, BF16)
    kv_other = swap(jnp.stack([part(key, 1 - bit), part(value, 1 - bit)]), 1)
    w_theirs = swap(part(out_weight, 1 - bit), 1)
    kv_own = jnp.stack([part(key, bit), part(value, bit)])
    w_mine = part(out_weight, bit)

    sizes = [length // 2, length // 2] + [2 * length >> level for level in range(2, seq_levels + 1)]
    shapes = [planes(rows, half, BF16) for rows in sizes]
    pooled = call(pool_body, meta, (kv_own, kv_other), shapes)
    next_own, next_other = pooled[:2]
    coarse = dict(zip(range(1, seq_levels), pooled[2:], strict=True))

    w_rows = jnp.where(
        bit == 0,
        jnp.concatenate([w_mine, w_theirs], axis=0),
        jnp.concatenate([w_theirs, w_mine], axis=0),
    )
    w_received = permute(w_rows, stages[0])
    far_masks = [(h, (1 << h) + (low << 3)) for h in range(3, seq_levels) for low in range(1 << (h - 3))]
    high_parts = [swap(coarse[h], mask) for h, mask in far_masks]
    first_panel = swap(coarse[1], 2)
    w_received, first_panel, *high_parts = lax.optimization_barrier(
        (w_received, first_panel, *high_parts)
    )

    high = jnp.concatenate(high_parts, axis=1)
    second = jnp.concatenate([coarse[2], high], axis=1)
    panels = [high, first_panel, swap(high, 2), swap(second, 4), swap(second, 6)]
    for stage in stages[1:-2]:
        w_rows = jnp.concatenate([w_rows, w_received], axis=0)
        w_received = permute(w_rows, stage)
    query, grad = lax.optimization_barrier((query, grad, high))[:2]
    q_other = swap(part(query, 1 - bit), 1)
    g_other = swap(part(grad, 1 - bit), 1)
    q_own = part(query, bit)
    g_own = part(grad, bit)
    n_high, n_second = high.shape[1], coarse[2].shape[1]
    parts = ((1, 0, coarse[1].shape[1]), (3, 0, n_second), (4, 0, n_second))
    parts += ((0, 0, n_high), (2, 0, n_high), (3, n_second, n_high), (4, n_second, n_high))

    w_rows = jnp.concatenate([w_rows, after(w_received, panels[2])], axis=0)
    w_received = permute(w_rows, stages[-2])
    w_last = permute(w_rows, stages[-1])

    key_count = length + length // 2 + sum(rows for _, _, rows in parts)
    att_ops = (q_own, q_other, kv_own, kv_other, next_own, next_other, *panels)
    attn_mine, probs = call(
        lambda *refs: forward_body(parts, *refs),
        after(meta, w_rows),
        att_ops,
        [struct(2 * length, half, BF16), jax.ShapeDtypeStruct((2 * heads, key_count, length), BF16)],
        flops=32 * 2 * length * key_count * half,
    )

    w_received, w_last, _ = lax.optimization_barrier((w_received, w_last, attn_mine))
    quarters = (w_rows, w_received, w_last, permute(w_received, stages[-1]))
    attn_theirs = swap(attn_mine, 1)

    scratch = [pltpu.VMEM((pieces * piece, cols), BF16)]
    wg = call(
        lambda *refs: weight_grad_body(piece, masks, *refs),
        meta,
        (attn_mine, attn_theirs, g_own, g_other),
        [struct(pieces * piece // 4, cols, BF16)] * 4,
        scratch,
    )
    wg_received = [permute(after(part, quarters[3]), stages[-1]) for part in (wg[3], wg[2])]

    d_keep, d_send = call(
        lambda *refs: d_attn_body(piece, masks, *refs),
        after(meta, wg[0]),
        (g_own, g_other, *quarters),
        [struct(2 * length, half, F32), struct(2 * length, half, BF16)],
        scratch,
    )
    d_recv = swap(d_send, 1)

    def add(kept, received):
        return (kept.astype(F32) + received.astype(F32)).astype(BF16)

    back_ops = att_ops + (d_keep, d_recv, probs)

    def backward(which, token, previous):
        width = which[-1] * HS + HS
        near_count = length + length // 2
        shapes = [struct(length, width, BF16)] * 2
        shapes += [planes(near_count, width, F32), planes(near_count, width, BF16)]
        shapes += [planes(p.shape[1], width, BF16) for p in panels]
        return call(
            lambda *refs: backward_body(parts, len(panels), len(shapes), which, *refs),
            token,
            back_ops + tuple(previous),
            shapes,
        )

    grads = backward(range(heads // 2), meta, ())
    wg_send = add(wg[1], after(wg_received[0], grads[0]))
    wg_step = permute(wg_send, stages[-2])
    grads = backward(range(heads // 2, heads), after(meta, wg_send), grads)
    wg_keep = add(wg[0], after(wg_received[1], grads[0]))
    wg_total = add(wg_keep, wg_step)
    wg_rows = wg_total.shape[0] // 2
    wg_keep, wg_send = wg_total[:wg_rows], wg_total[wg_rows:]
    grads = lax.optimization_barrier((*grads, wg_send))[: len(grads)]
    dq_keep, dq_send, near_keep, near_send, high_own, first_grad, *rest = grads

    back = [swap(part, mask) for part, mask in zip(rest, (2, 4, 6), strict=True)]
    first_back = swap(first_grad, 2)
    wg_received = permute(wg_send, stages[-3])
    at_meta = after(meta, high_own)
    near_recv = swap(near_send, 1)
    dq_recv = swap(dq_send, 1)
    base_k, base_v = call(near_body, meta, (near_keep, near_recv), [struct(length, inner, F32)] * 2)

    at_keep, at_send = call(
        lambda *refs: attended_body(piece, masks, *refs),
        at_meta,
        (attn_mine, attn_theirs, *quarters),
        [g_half, g_half],
        scratch,
    )
    grad_queries, attended = call(
        place_body,
        meta,
        (dq_keep, dq_recv, at_keep, swap(at_send, 1)),
        [struct(length, inner, BF16), struct(length, 2 * cols, BF16)],
        last=True,
    )

    wg_received, first_back, *back = lax.optimization_barrier(
        (wg_received, first_back, *back, base_k, base_v, attended, grad_queries)
    )[: 2 + len(back)]
    wg_total = add(wg_keep, wg_received)
    wg_rows = wg_total.shape[0] // 2
    wg_keep, wg_send = wg_total[:wg_rows], wg_total[wg_rows:]
    wg_received = permute(wg_send, stages[-4])
    cuts = [coarse[h].shape[1] for h, _ in far_masks]
    high_shapes = [planes(rows, half, BF16) for rows in cuts]
    high_sums = call(
        lambda *refs: high_body(cuts, (0, n_second, n_second), *refs),
        after(meta, wg_send),
        (high_own, *back),
        high_shapes,
    )
    by_level = {1: [first_back], 2: back[1:]}
    for (h, mask), part in zip(far_masks, high_sums, strict=True):
        by_level.setdefault(h, []).append(swap(part, mask))
    total = wg_keep.astype(F32) + wg_received.astype(F32)
    rows = piece // 2
    wg_mine = lax.dynamic_slice_in_dim(total, bit * rows, rows, 0)
    wg_theirs = swap(lax.dynamic_slice_in_dim(total, (1 - bit) * rows, rows, 0).astype(BF16), 1)
    wg_theirs = wg_theirs.astype(F32)
    weight_grad = jnp.where(
        bit == 0,
        jnp.concatenate([wg_mine, wg_theirs], axis=1),
        jnp.concatenate([wg_theirs, wg_mine], axis=1),
    )
    if dp_count > 1:
        weight_grad = lax.psum_scatter(
            weight_grad.astype(BF16), "dp", scatter_dimension=1, tiled=True
        ).astype(F32)
    weight_grad = weight_grad * (1.0 / math.sqrt(token_total))

    levels = list(reversed(range(1, seq_levels)))
    received = [part for h in levels for part in by_level[h]]
    counts = [len(by_level[h]) for h in levels]
    up_rows = coarse[1].shape[1] // 2
    up_keep, up_send = call(
        lambda *refs: cascade_body(counts, *refs),
        after(meta, weight_grad),
        received,
        [planes(up_rows, half, F32), planes(up_rows, half, BF16)],
    )
    grad_keys, grad_values = call(
        finish_body,
        meta,
        (base_k, base_v, up_keep, swap(up_send, 1)),
        [struct(length, inner, BF16)] * 2,
        last=True,
    )
    return (attended[None], grad_queries[None], grad_keys[None], grad_values[None], weight_grad)


def solution(mesh):
    placed = (
        P("dp", "seq", None),
        P("dp", "seq", None),
        P("dp", "seq", None),
        P("seq", "dp"),
        P("dp", "seq", None),
    )
    return jax.shard_map(
        body,
        mesh=mesh,
        in_specs=placed,
        out_specs=(
            P("dp", "seq", None),
            P("dp", "seq", None),
            P("dp", "seq", None),
            P("dp", "seq", None),
            P("seq", "dp"),
        ),
        check_vma=False,
    )
```

```python
import math

import jax
import jax.numpy as jnp
from jax import lax
from jax.experimental import pallas as pl
from jax.experimental.pallas import tpu as pltpu
from jax.sharding import PartitionSpec as P

HEADS = 8
HS = 128
NR = 128

HALF_ROOT = 0.7071067811865476
SCORE_SCALE = 1.0 / math.sqrt(HS)
EXP2_SCALE = SCORE_SCALE * math.log2(math.e)
F32 = jnp.float32
BF16 = jnp.bfloat16
VMEM_LIMIT = 20 * 1024 * 1024


def permute(value, masks):
    count = lax.axis_size("seq")
    return lax.ppermute(value, "seq", [(i, i ^ masks[i & 1]) for i in range(count)])


def swap(value, mask):
    return permute(value, (mask, mask))


def after(value, *others):
    return lax.optimization_barrier((value, *others))[0]


def call(body, meta, operands, shapes, scratch=(), last=False, flops=0):
    specs = [pl.BlockSpec(memory_space=pltpu.VMEM) for _ in operands]
    if last:
        out_specs = [pl.BlockSpec(s.shape, lambda i: (0,) * len(s.shape)) for s in shapes]
    else:
        out_specs = [pl.BlockSpec(memory_space=pltpu.VMEM) for _ in shapes]
    return pl.pallas_call(
        body,
        grid=(1,) if last else (),
        in_specs=[pl.BlockSpec(memory_space=pltpu.SMEM)] + specs,
        out_specs=out_specs,
        out_shape=shapes,
        scratch_shapes=list(scratch),
        compiler_params=pltpu.CompilerParams(vmem_limit_bytes=VMEM_LIMIT),
        cost_estimate=pl.CostEstimate(flops=flops, bytes_accessed=0, transcendentals=0),
    )(meta, *operands)


def struct(rows, cols, dtype):
    return jax.ShapeDtypeStruct((rows, cols), dtype)


def planes(rows, cols, dtype):
    return jax.ShapeDtypeStruct((2, rows, cols), dtype)


def dot(a, b, dims):
    return lax.dot_general(a, b, (dims, ((), ())), preferred_element_type=F32)


NN = ((1,), (0,))
NT = ((1,), (1,))
TN = ((0,), (0,))


def group_matrix(rows, cols, row_div, col_div):
    row = lax.broadcasted_iota(jnp.int32, (rows, cols), 0) // row_div
    col = lax.broadcasted_iota(jnp.int32, (rows, cols), 1) // col_div
    return jnp.where(row == col, 1.0, 0.0).astype(BF16)


def pool(rows):
    half = rows.shape[0] // 2
    return (dot(group_matrix(half, 2 * half, 1, 2), rows, NN) * HALF_ROOT).astype(BF16)


def spread(grad, times, factor):
    high = grad.astype(BF16)
    low = (grad - high.astype(F32)).astype(BF16)
    matrix = group_matrix(times * grad.shape[0], grad.shape[0], times, 1)
    return (dot(matrix, high, NN) + dot(matrix, low, NN)) * factor


def lanes(ref):
    return jnp.concatenate([ref[0], ref[1]], axis=1)


def put_planes(ref, rows):
    width = ref.shape[2]
    ref[0] = rows[:, :width].astype(ref.dtype)
    ref[1] = rows[:, width:].astype(ref.dtype)


def half_of(meta, width, mine):
    start = meta[0] * width if mine else (1 - meta[0]) * width
    return pl.ds(pl.multiple_of(start, width), width)


def pool_body(meta, own, other, *outs):
    first_own = pool(lanes(own))
    first_other = pool(lanes(other))
    put_planes(outs[0], first_own)
    put_planes(outs[1], first_other)
    rows = jnp.concatenate([pool(first_own), pool(first_other)], axis=0)
    put_planes(outs[2], rows)
    for out in outs[3:]:
        rows = pool(rows)
        put_planes(out, rows)


def key_sets(kv_own, kv_other, next_own, next_other, far, at):
    near = (kv_own, kv_other)
    coarse = (next_other, next_own)
    sets = []
    for plane in range(2):
        far_rows = [ref[plane, start : start + rows, at] for ref, start, rows in far]
        sets.append(
            [
                jnp.concatenate([near[group][plane, :, at], coarse[group][plane, :, at]] + far_rows, axis=0)
                for group in range(2)
            ]
        )
    return sets


def forward_body(parts, meta, q_own, q_other, kv_own, kv_other, next_own, next_other, *refs):
    attn_ref, probs_ref = refs[-2:]
    far = [(refs[index], start, rows) for index, start, rows in parts]
    length, width = q_own.shape
    chunk = length // 2
    for head in range(width // HS):
        at = slice(head * HS, (head + 1) * HS)
        keys, values = key_sets(kv_own, kv_other, next_own, next_other, far, at)
        for group, q_ref in enumerate((q_own, q_other)):
            scores = dot(keys[group], q_ref[:, at], NT)
            for start in range(0, length, chunk):
                some = scores[:, start : start + chunk]
                top = jnp.max(some, axis=0, keepdims=True)
                weights = jnp.exp2((some - top) * EXP2_SCALE)
                total = jnp.sum(weights, axis=0, keepdims=True)
                probs = (weights * (1.0 / total)).astype(BF16)
                probs_ref[2 * head + group, :, start : start + chunk] = probs
                first = group * length + start
                attn_ref[first : first + chunk, at] = dot(probs, values[group], TN).astype(BF16)


def backward_body(
    parts, n_far, meta, q_own, q_other, kv_own, kv_other, next_own, next_other, *refs
):
    far = [(refs[index], start, rows) for index, start, rows in parts]
    d_keep, d_recv, probs_ref, dq_own, dq_other, near_own, near_other, *far_grads = refs[n_far:]
    near_rows = kv_own.shape[1]
    after_next = near_rows + next_own.shape[1]
    for head in range(q_own.shape[1] // HS):
        at = slice(head * HS, (head + 1) * HS)
        keys, values = key_sets(kv_own, kv_other, next_own, next_other, far, at)
        grads = ([], [])
        for group, (q_ref, dq_ref) in enumerate(((q_own, dq_own), (q_other, dq_other))):
            length = q_ref.shape[0]
            rows = slice(group * length, (group + 1) * length)
            d_attn = (d_keep[rows, at] + d_recv[rows, at].astype(F32)).astype(BF16)
            probs_low = probs_ref[2 * head + group]
            probs = probs_low.astype(F32)
            d_prob = dot(values[group], d_attn, NT)
            center = jnp.sum(probs * d_prob, axis=0, keepdims=True)
            d_score = (probs * (d_prob - center)).astype(BF16)
            dq_ref[:, at] = (dot(d_score, keys[group], TN) * SCORE_SCALE).astype(BF16)
            grads[0].append(dot(d_score, q_ref[:, at], NN))
            grads[1].append(dot(probs_low, d_attn, NN))
        for plane, factor in enumerate((SCORE_SCALE, 1.0)):
            for group, near in enumerate((near_own, near_other)):
                mine, other = grads[plane][group], grads[plane][1 - group]
                near[plane, :near_rows, at] = (mine[:near_rows] * factor).astype(near.dtype)
                near[plane, near_rows:, at] = (other[near_rows:after_next] * factor).astype(near.dtype)
            total = (grads[plane][0][after_next:] + grads[plane][1][after_next:]) * factor
            done = 0
            for index, start, rows in parts:
                out = far_grads[index]
                out[plane, start : start + rows, at] = total[done : done + rows].astype(BF16)
                done += rows


def pieces_of(parts, piece, masks, meta):
    for half in range(2):
        width = parts[0].shape[1]
        columns = slice(half * width, (half + 1) * width)
        index = 0
        for part in parts[2 * half : 2 * half + 2]:
            for start in range(0, part.shape[0], piece):
                first, second = masks[half][0][index], masks[half][1][index]
                owner = meta[1] ^ jnp.where(meta[0] == 0, first, second)
                rows = pl.ds(pl.multiple_of(owner * piece, piece), piece)
                yield part, slice(start, start + piece), rows, columns
                index += 1


def ordered_weight(meta, parts, scratch, piece, masks):
    for part, there, rows, columns in pieces_of(parts, piece, masks, meta):
        scratch[rows, columns] = part[there, :]


def d_attn_body(piece, masks, meta, grad_own, grad_other, *refs):
    keep, send, scratch = refs[-3:]
    ordered_weight(meta, refs[:-3], scratch, piece, masks)
    length = grad_own.shape[0]
    mine = scratch[half_of(meta, keep.shape[1], True), :]
    theirs = scratch[half_of(meta, keep.shape[1], False), :]
    send[:length] = dot(grad_other[...], theirs, NT).astype(BF16)
    send[length:] = dot(grad_own[...], theirs, NT).astype(BF16)
    keep[:length] = dot(grad_own[...], mine, NT)
    keep[length:] = dot(grad_other[...], mine, NT)


def attended_body(piece, masks, meta, attn_mine, attn_theirs, *refs):
    keep, send, scratch = refs[-3:]
    ordered_weight(meta, refs[:-3], scratch, piece, masks)
    length = keep.shape[0]
    mine = scratch[half_of(meta, attn_mine.shape[1], True), :]
    theirs = scratch[half_of(meta, attn_mine.shape[1], False), :]
    send[...] = (
        dot(attn_mine[length:], mine, NN) + dot(attn_theirs[:length], theirs, NN)
    ).astype(BF16)
    keep[...] = (
        dot(attn_mine[:length], mine, NN) + dot(attn_theirs[length:], theirs, NN)
    ).astype(BF16)


def weight_grad_body(piece, masks, meta, attn_mine, attn_theirs, grad_own, grad_other, *refs):
    scratch = refs[-1]
    length = grad_own.shape[0]
    width = attn_mine.shape[1]
    mine = dot(attn_mine[:length], grad_own[...], TN) + dot(attn_mine[length:], grad_other[...], TN)
    scratch[half_of(meta, width, True), :] = mine.astype(BF16)
    theirs = dot(attn_theirs[length:], grad_own[...], TN) + dot(
        attn_theirs[:length], grad_other[...], TN
    )
    scratch[half_of(meta, width, False), :] = theirs.astype(BF16)
    for part, there, rows, columns in pieces_of(refs[:-1], piece, masks, meta):
        part[there, :] = scratch[rows, columns]


def high_body(cuts, skips, meta, own, *refs):
    received = refs[: len(skips)]
    for plane in range(2):
        total = own[plane].astype(F32)
        for ref, skip in zip(received, skips, strict=True):
            total = total + ref[plane, skip:].astype(F32)
        start = 0
        for out, rows in zip(refs[len(skips) :], cuts, strict=True):
            out[plane] = total[start : start + rows].astype(BF16)
            start += rows


def cascade_body(counts, meta, *refs):
    keep, send = refs[-2:]
    half = keep.shape[1]
    total = None
    start = 0
    rows = 2 * half >> (len(counts) - 1)
    for count in counts:
        level = lanes(refs[start])[:rows].astype(F32)
        for ref in refs[start + 1 : start + count]:
            level = level + lanes(ref)[:rows].astype(F32)
        start += count
        rows *= 2
        total = level if total is None else level + spread(total, 2, HALF_ROOT)
    put_planes(keep, total[:half])
    put_planes(send, total[half:])


def near_body(meta, keep, recv, dk, dv):
    rows, width = dk.shape[0], keep.shape[2]
    matrix = group_matrix(rows, keep.shape[1] - rows, 2, 1)
    for plane, out in enumerate((dk, dv)):
        own = keep[plane, :rows] + spread(keep[plane, rows:], 2, HALF_ROOT)
        out[:, half_of(meta, width, True)] = own
        other = recv[plane, :rows].astype(F32) + dot(matrix, recv[plane, rows:], NN) * HALF_ROOT
        out[:, half_of(meta, width, False)] = other


def finish_body(meta, base_k, base_v, up_keep, up_recv, dk, dv):
    rows, width = dk.shape[0], up_keep.shape[2]
    times = rows // up_keep.shape[1]
    factor = HALF_ROOT * HALF_ROOT
    matrix = group_matrix(rows, up_recv.shape[1], times, 1)
    mine, theirs = half_of(meta, width, True), half_of(meta, width, False)
    for plane, (base, out) in enumerate(((base_k, dk), (base_v, dv))):
        out[:, mine] = (base[:, mine] + spread(up_keep[plane], times, factor)).astype(BF16)
        received = dot(matrix, up_recv[plane], NN) * factor
        out[:, theirs] = (base[:, theirs] + received).astype(BF16)


def place_body(meta, *refs):
    outs = refs[2 * len(refs) // 3 :]
    for index, out in enumerate(outs):
        width = out.shape[1] // 2
        out[:, half_of(meta, width, True)] = refs[2 * index][...]
        out[:, half_of(meta, width, False)] = refs[2 * index + 1][...]


def body(queries, keys, values, out_weight, out_grad):
    inner = queries.shape[2]
    half = inner // 2
    length = queries.shape[1]
    heads = HEADS // 2
    seq_count = lax.axis_size("seq")
    seq_levels = seq_count.bit_length() - 1
    dp_count = lax.axis_size("dp")
    rank = lax.axis_index("seq")
    bit = rank % 2
    pair = rank // 2
    token_total = length * seq_count * queries.shape[0] * dp_count

    up = [1 << level for level in reversed(range(1, seq_levels))]
    pieces = seq_count // 2

    def halves_of(orders):
        both = [orders, [order[:-2] + order[:-3:-1] for order in orders]]
        masks = [
            [
                [sum(m for s, m in enumerate(order) if index >> s & 1) // 2 for index in range(pieces)]
                for order in one
            ]
            for one in both
        ]
        return [list(zip(*one, strict=True)) for one in both], masks

    stages, masks = halves_of([up[:-2] + [2, 4], [2] + up[:-3] + [4, 8]])
    sum_stages, sum_masks = halves_of([up[:-3] + [4, 8, 2], [2] + up[:-3] + [8, 4]])
    meta = jnp.stack([bit, pair]).astype(jnp.int32)

    query = queries[0]
    key = keys[0]
    value = values[0]
    grad = out_grad[0]
    if dp_count > 1:
        out_weight = lax.all_gather(out_weight, "dp", axis=1, tiled=True)
    cols = out_weight.shape[1] // 2
    piece = 2 * out_weight.shape[0]

    def part(array, which):
        width = array.shape[1] // 2
        return lax.dynamic_slice_in_dim(array, which * width, width, 1)

    q_half = struct(length, half, BF16)
    g_half = struct(length, cols, BF16)
    kv_other = swap(jnp.stack([part(key, 1 - bit), part(value, 1 - bit)]), 1)
    w_theirs = swap(part(out_weight, 1 - bit), 1)
    kv_own = jnp.stack([part(key, bit), part(value, bit)])
    w_mine = part(out_weight, bit)

    sizes = [length // 2, length // 2] + [2 * length >> level for level in range(2, seq_levels + 1)]
    shapes = [planes(rows, half, BF16) for rows in sizes]
    pooled = call(pool_body, meta, (kv_own, kv_other), shapes)
    next_own, next_other = pooled[:2]
    coarse = dict(zip(range(1, seq_levels), pooled[2:], strict=True))

    w_rows = jnp.where(
        bit == 0,
        jnp.concatenate([w_mine, w_theirs], axis=0),
        jnp.concatenate([w_theirs, w_mine], axis=0),
    )
    w_received = permute(w_rows, stages[0][0])
    far_masks = [(h, (1 << h) + (low << 3)) for h in range(3, seq_levels) for low in range(1 << (h - 3))]
    high_parts = [swap(coarse[h], mask) for h, mask in far_masks]
    first_panel = swap(coarse[1], 2)
    w_received, first_panel, *high_parts = lax.optimization_barrier(
        (w_received, first_panel, *high_parts)
    )

    high = jnp.concatenate(high_parts, axis=1)
    second = jnp.concatenate([coarse[2], high], axis=1)
    panels = [high, first_panel, swap(high, 2), swap(second, 4), swap(second, 6)]
    for stage in stages[0][1:-2]:
        w_rows = jnp.concatenate([w_rows, w_received], axis=0)
        w_received = permute(w_rows, stage)
    query, grad = lax.optimization_barrier((query, grad, high))[:2]
    q_other = swap(part(query, 1 - bit), 1)
    g_other = swap(part(grad, 1 - bit), 1)
    q_own = part(query, bit)
    g_own = part(grad, bit)
    n_high, n_second = high.shape[1], coarse[2].shape[1]
    parts = ((1, 0, coarse[1].shape[1]), (3, 0, n_second), (4, 0, n_second))
    parts += ((0, 0, n_high), (2, 0, n_high), (3, n_second, n_high), (4, n_second, n_high))

    w_received = after(w_received, panels[2])
    w_width = cols // 2
    w_rows = [
        jnp.concatenate([rows[:, start : start + w_width] for rows in (w_rows, w_received)], axis=0)
        for start in (0, w_width)
    ]
    w_received = [permute(rows, order[-2]) for rows, order in zip(w_rows, stages, strict=True)]

    key_count = length + length // 2 + sum(rows for _, _, rows in parts)
    att_ops = (q_own, q_other, kv_own, kv_other, next_own, next_other, *panels)
    attn_mine, probs = call(
        lambda *refs: forward_body(parts, *refs),
        after(meta, *w_rows),
        att_ops,
        [struct(2 * length, half, BF16), jax.ShapeDtypeStruct((2 * heads, key_count, length), BF16)],
        flops=32 * 2 * length * key_count * half,
    )

    w_received = lax.optimization_barrier((*w_received, attn_mine))[:2]
    w_rows = [jnp.concatenate(rows, axis=0) for rows in zip(w_rows, w_received, strict=True)]
    w_received = [permute(rows, order[-1]) for rows, order in zip(w_rows, stages, strict=True)]
    quarters = (w_rows[0], w_received[0], w_rows[1], w_received[1])
    attn_theirs = swap(attn_mine, 1)

    scratch = [pltpu.VMEM((pieces * piece, cols), BF16)]
    wg = call(
        lambda *refs: weight_grad_body(piece, sum_masks, *refs),
        meta,
        (attn_mine, attn_theirs, g_own, g_other),
        [struct(pieces * piece // 2, w_width, BF16)] * 4,
        scratch,
    )
    wg_send = lax.optimization_barrier((wg[1], wg[3], *w_received))[:2]
    wg_received = [permute(part, order[-1]) for part, order in zip(wg_send, sum_stages, strict=True)]

    d_keep, d_send = call(
        lambda *refs: d_attn_body(piece, masks, *refs),
        after(meta, wg[0]),
        (g_own, g_other, *quarters),
        [struct(2 * length, half, F32), struct(2 * length, half, BF16)],
        scratch,
    )
    d_recv = swap(d_send, 1)

    back_ops = att_ops + (d_keep, d_recv, probs)

    near_count = length + length // 2
    grad_shapes = [q_half, q_half, planes(near_count, half, F32), planes(near_count, half, BF16)]
    grad_shapes += [planes(p.shape[1], half, BF16) for p in panels]
    grads = call(
        lambda *refs: backward_body(parts, len(panels), *refs),
        meta,
        att_ops + (d_keep, d_recv, probs),
        grad_shapes,
    )
    dq_keep, dq_send, near_keep, near_send, high_own, first_grad, *rest = grads

    back = [swap(part, mask) for part, mask in zip(rest, (2, 4, 6), strict=True)]
    first_back = swap(first_grad, 2)

    def add(kept, received):
        return (kept.astype(F32) + received.astype(F32)).astype(BF16)

    def add_halves(kept, received):
        total = add(kept, received)
        rows = total.shape[0] // 2
        return total[:rows], total[rows:]

    wg_received = lax.optimization_barrier((*wg_received, back[0]))[:2]
    wg_keep, wg_send = zip(*map(add_halves, (wg[0], wg[2]), wg_received), strict=True)
    wg_received = [permute(part, order[-2]) for part, order in zip(wg_send, sum_stages, strict=True)]
    at_meta = after(meta, *wg_send)
    near_recv = swap(near_send, 1)
    dq_recv = swap(dq_send, 1)
    base_k, base_v = call(near_body, meta, (near_keep, near_recv), [struct(length, inner, F32)] * 2)

    at_keep, at_send = call(
        lambda *refs: attended_body(piece, masks, *refs),
        at_meta,
        (attn_mine, attn_theirs, *quarters),
        [g_half, g_half],
        scratch,
    )
    first_back, *others = lax.optimization_barrier(
        (first_back, *back, *wg_received, base_k, base_v, at_keep)
    )
    back, wg_received = others[: len(back)], others[len(back) : len(back) + 2]
    wg_total = jnp.concatenate([add(*both) for both in zip(wg_keep, wg_received, strict=True)], axis=1)
    wg_rows = wg_total.shape[0] // 2
    wg_keep, wg_send = wg_total[:wg_rows], wg_total[wg_rows:]
    wg_received = permute(wg_send, sum_stages[0][-3])
    grad_queries, attended = call(
        place_body,
        meta,
        (dq_keep, dq_recv, at_keep, swap(after(at_send, wg_total), 1)),
        [struct(length, inner, BF16), struct(length, 2 * cols, BF16)],
        last=True,
    )
    cuts = [coarse[h].shape[1] for h, _ in far_masks]
    high_shapes = [planes(rows, half, BF16) for rows in cuts]
    high_sums = call(
        lambda *refs: high_body(cuts, (0, n_second, n_second), *refs),
        meta,
        (high_own, *back),
        high_shapes,
    )
    by_level = {1: [first_back], 2: back[1:]}
    high_back = [swap(part, mask) for (_, mask), part in zip(far_masks, high_sums, strict=True)]
    *high_back, wg_received = lax.optimization_barrier((*high_back, wg_received))
    wg_keep, wg_send = add_halves(wg_keep, wg_received)
    wg_received = permute(wg_send, sum_stages[0][-4])
    for (h, _), part in zip(far_masks, high_back, strict=True):
        by_level.setdefault(h, []).append(part)
    levels = list(reversed(range(1, seq_levels)))
    received = [part for h in levels for part in by_level[h]]
    counts = [len(by_level[h]) for h in levels]
    up_rows = coarse[1].shape[1] // 2
    up_keep, up_send = call(
        lambda *refs: cascade_body(counts, *refs),
        after(meta, wg_send),
        received,
        [planes(up_rows, half, F32), planes(up_rows, half, BF16)],
    )
    wg_received = after(wg_received, up_keep, attended)
    total = wg_keep.astype(F32) + wg_received.astype(F32)
    rows = piece // 2
    wg_mine = lax.dynamic_slice_in_dim(total, bit * rows, rows, 0)
    wg_theirs = swap(lax.dynamic_slice_in_dim(total, (1 - bit) * rows, rows, 0).astype(BF16), 1)
    wg_theirs = wg_theirs.astype(F32)
    weight_grad = jnp.where(
        bit == 0,
        jnp.concatenate([wg_mine, wg_theirs], axis=1),
        jnp.concatenate([wg_theirs, wg_mine], axis=1),
    )
    if dp_count > 1:
        weight_grad = lax.psum_scatter(
            weight_grad.astype(BF16), "dp", scatter_dimension=1, tiled=True
        ).astype(F32)
    weight_grad = weight_grad * (1.0 / math.sqrt(token_total))
    grad_keys, grad_values = call(
        finish_body,
        meta,
        (base_k, base_v, up_keep, swap(up_send, 1)),
        [struct(length, inner, BF16)] * 2,
        last=True,
    )
    return (attended[None], grad_queries[None], grad_keys[None], grad_values[None], weight_grad)


def solution(mesh):
    placed = (
        P("dp", "seq", None),
        P("dp", "seq", None),
        P("dp", "seq", None),
        P("seq", "dp"),
        P("dp", "seq", None),
    )
    return jax.shard_map(
        body,
        mesh=mesh,
        in_specs=placed,
        out_specs=(
            P("dp", "seq", None),
            P("dp", "seq", None),
            P("dp", "seq", None),
            P("dp", "seq", None),
            P("seq", "dp"),
        ),
        check_vma=False,
    )
```

```python
import math

import jax
import jax.numpy as jnp
from jax import lax
from jax.experimental import pallas as pl
from jax.experimental.pallas import tpu as pltpu
from jax.sharding import PartitionSpec as P

HEADS = 8
HS = 128
NR = 128

HALF_ROOT = 0.7071067811865476
SCORE_SCALE = 1.0 / math.sqrt(HS)
EXP2_SCALE = SCORE_SCALE * math.log2(math.e)
F32 = jnp.float32
BF16 = jnp.bfloat16
VMEM_LIMIT = 20 * 1024 * 1024


def permute(value, masks):
    count = lax.axis_size("seq")
    return lax.ppermute(value, "seq", [(i, i ^ masks[i & 1]) for i in range(count)])


def swap(value, mask):
    return permute(value, (mask, mask))


def after(value, *others):
    return lax.optimization_barrier((value, *others))[0]


def call(body, meta, operands, shapes, scratch=(), last=False, flops=0):
    specs = [pl.BlockSpec(memory_space=pltpu.VMEM) for _ in operands]
    if last:
        out_specs = [pl.BlockSpec(s.shape, lambda i: (0,) * len(s.shape)) for s in shapes]
    else:
        out_specs = [pl.BlockSpec(memory_space=pltpu.VMEM) for _ in shapes]
    return pl.pallas_call(
        body,
        grid=(1,) if last else (),
        in_specs=[pl.BlockSpec(memory_space=pltpu.SMEM)] + specs,
        out_specs=out_specs,
        out_shape=shapes,
        scratch_shapes=list(scratch),
        compiler_params=pltpu.CompilerParams(vmem_limit_bytes=VMEM_LIMIT),
        cost_estimate=pl.CostEstimate(flops=flops, bytes_accessed=0, transcendentals=0),
    )(meta, *operands)


def struct(rows, cols, dtype):
    return jax.ShapeDtypeStruct((rows, cols), dtype)


def planes(rows, cols, dtype):
    return jax.ShapeDtypeStruct((2, rows, cols), dtype)


def dot(a, b, dims):
    return lax.dot_general(a, b, (dims, ((), ())), preferred_element_type=F32)


NN = ((1,), (0,))
NT = ((1,), (1,))
TN = ((0,), (0,))


def group_matrix(rows, cols, row_div, col_div):
    row = lax.broadcasted_iota(jnp.int32, (rows, cols), 0) // row_div
    col = lax.broadcasted_iota(jnp.int32, (rows, cols), 1) // col_div
    return jnp.where(row == col, 1.0, 0.0).astype(BF16)


def pool(rows):
    half = rows.shape[0] // 2
    return (dot(group_matrix(half, 2 * half, 1, 2), rows, NN) * HALF_ROOT).astype(BF16)


def spread(grad, times, factor):
    high = grad.astype(BF16)
    low = (grad - high.astype(F32)).astype(BF16)
    matrix = group_matrix(times * grad.shape[0], grad.shape[0], times, 1)
    return (dot(matrix, high, NN) + dot(matrix, low, NN)) * factor


def lanes(ref):
    return jnp.concatenate([ref[0], ref[1]], axis=1)


def put_planes(ref, rows):
    width = ref.shape[2]
    ref[0] = rows[:, :width].astype(ref.dtype)
    ref[1] = rows[:, width:].astype(ref.dtype)


def half_of(meta, width, mine):
    start = meta[0] * width if mine else (1 - meta[0]) * width
    return pl.ds(pl.multiple_of(start, width), width)


def pool_body(meta, own, other, *outs):
    first_own = pool(lanes(own))
    first_other = pool(lanes(other))
    put_planes(outs[0], first_own)
    put_planes(outs[1], first_other)
    rows = jnp.concatenate([pool(first_own), pool(first_other)], axis=0)
    put_planes(outs[2], rows)
    for out in outs[3:]:
        rows = pool(rows)
        put_planes(out, rows)


def key_sets(kv_own, kv_other, next_own, next_other, far, at):
    near = (kv_own, kv_other)
    coarse = (next_other, next_own)
    sets = []
    for plane in range(2):
        far_rows = [ref[plane, start : start + rows, at] for ref, start, rows in far]
        sets.append(
            [
                jnp.concatenate([near[group][plane, :, at], coarse[group][plane, :, at]] + far_rows, axis=0)
                for group in range(2)
            ]
        )
    return sets


def forward_body(parts, meta, q_own, q_other, kv_own, kv_other, next_own, next_other, *refs):
    attn_ref, probs_ref = refs[-2:]
    far = [(refs[index], start, rows) for index, start, rows in parts]
    length, width = q_own.shape
    chunk = length // 2
    for head in range(width // HS):
        at = slice(head * HS, (head + 1) * HS)
        keys, values = key_sets(kv_own, kv_other, next_own, next_other, far, at)
        for group, q_ref in enumerate((q_own, q_other)):
            scores = dot(keys[group], q_ref[:, at], NT)
            for start in range(0, length, chunk):
                some = scores[:, start : start + chunk]
                top = jnp.max(some, axis=0, keepdims=True)
                weights = jnp.exp2((some - top) * EXP2_SCALE)
                total = jnp.sum(weights, axis=0, keepdims=True)
                probs = (weights * (1.0 / total)).astype(BF16)
                probs_ref[2 * head + group, :, start : start + chunk] = probs
                first = group * length + start
                attn_ref[first : first + chunk, at] = dot(probs, values[group], TN).astype(BF16)


def backward_body(
    parts, n_far, meta, q_own, q_other, kv_own, kv_other, next_own, next_other, *refs
):
    far = [(refs[index], start, rows) for index, start, rows in parts]
    d_keep, d_recv, probs_ref, dq_own, dq_other, near_own, near_other, *far_grads = refs[n_far:]
    near_rows = kv_own.shape[1]
    after_next = near_rows + next_own.shape[1]
    for head in range(q_own.shape[1] // HS):
        at = slice(head * HS, (head + 1) * HS)
        keys, values = key_sets(kv_own, kv_other, next_own, next_other, far, at)
        grads = ([], [])
        for group, (q_ref, dq_ref) in enumerate(((q_own, dq_own), (q_other, dq_other))):
            length = q_ref.shape[0]
            rows = slice(group * length, (group + 1) * length)
            d_attn = (d_keep[rows, at] + d_recv[rows, at].astype(F32)).astype(BF16)
            probs_low = probs_ref[2 * head + group]
            probs = probs_low.astype(F32)
            d_prob = dot(values[group], d_attn, NT)
            center = jnp.sum(probs * d_prob, axis=0, keepdims=True)
            d_score = (probs * (d_prob - center)).astype(BF16)
            dq_ref[:, at] = (dot(d_score, keys[group], TN) * SCORE_SCALE).astype(BF16)
            grads[0].append(dot(d_score, q_ref[:, at], NN))
            grads[1].append(dot(probs_low, d_attn, NN))
        for plane, factor in enumerate((SCORE_SCALE, 1.0)):
            for group, near in enumerate((near_own, near_other)):
                mine, other = grads[plane][group], grads[plane][1 - group]
                near[plane, :near_rows, at] = (mine[:near_rows] * factor).astype(near.dtype)
                near[plane, near_rows:, at] = (other[near_rows:after_next] * factor).astype(near.dtype)
            total = (grads[plane][0][after_next:] + grads[plane][1][after_next:]) * factor
            done = 0
            for index, start, rows in parts:
                out = far_grads[index]
                out[plane, start : start + rows, at] = total[done : done + rows].astype(BF16)
                done += rows


def pieces_of(parts, piece, masks, meta):
    for half in range(2):
        width = parts[0].shape[1]
        columns = slice(half * width, (half + 1) * width)
        index = 0
        for part in parts[2 * half : 2 * half + 2]:
            for start in range(0, part.shape[0], piece):
                first, second = masks[half][0][index], masks[half][1][index]
                owner = meta[1] ^ jnp.where(meta[0] == 0, first, second)
                rows = pl.ds(pl.multiple_of(owner * piece, piece), piece)
                yield part, slice(start, start + piece), rows, columns
                index += 1


def ordered_weight(meta, parts, scratch, piece, masks):
    for part, there, rows, columns in pieces_of(parts, piece, masks, meta):
        scratch[rows, columns] = part[there, :]


def d_attn_body(piece, masks, meta, grad_own, grad_other, *refs):
    keep, send, scratch = refs[-3:]
    ordered_weight(meta, refs[:-3], scratch, piece, masks)
    length = grad_own.shape[0]
    mine = scratch[half_of(meta, keep.shape[1], True), :]
    theirs = scratch[half_of(meta, keep.shape[1], False), :]
    send[:length] = dot(grad_other[...], theirs, NT).astype(BF16)
    send[length:] = dot(grad_own[...], theirs, NT).astype(BF16)
    keep[:length] = dot(grad_own[...], mine, NT)
    keep[length:] = dot(grad_other[...], mine, NT)


def attended_body(piece, masks, meta, attn_mine, attn_theirs, *refs):
    keep, send, scratch = refs[-3:]
    ordered_weight(meta, refs[:-3], scratch, piece, masks)
    length = keep.shape[0]
    mine = scratch[half_of(meta, attn_mine.shape[1], True), :]
    theirs = scratch[half_of(meta, attn_mine.shape[1], False), :]
    send[...] = (
        dot(attn_mine[length:], mine, NN) + dot(attn_theirs[:length], theirs, NN)
    ).astype(BF16)
    keep[...] = (
        dot(attn_mine[:length], mine, NN) + dot(attn_theirs[length:], theirs, NN)
    ).astype(BF16)


def weight_grad_body(piece, masks, meta, attn_mine, attn_theirs, grad_own, grad_other, *refs):
    scratch = refs[-1]
    length = grad_own.shape[0]
    width = attn_mine.shape[1]
    mine = dot(attn_mine[:length], grad_own[...], TN) + dot(attn_mine[length:], grad_other[...], TN)
    scratch[half_of(meta, width, True), :] = mine.astype(BF16)
    theirs = dot(attn_theirs[length:], grad_own[...], TN) + dot(
        attn_theirs[:length], grad_other[...], TN
    )
    scratch[half_of(meta, width, False), :] = theirs.astype(BF16)
    for part, there, rows, columns in pieces_of(refs[:-1], piece, masks, meta):
        part[there, :] = scratch[rows, columns]


def high_body(cuts, skips, meta, own, *refs):
    received = refs[: len(skips)]
    for plane in range(2):
        total = own[plane].astype(F32)
        for ref, skip in zip(received, skips, strict=True):
            total = total + ref[plane, skip:].astype(F32)
        start = 0
        for out, rows in zip(refs[len(skips) :], cuts, strict=True):
            out[plane] = total[start : start + rows].astype(BF16)
            start += rows


def add_body(meta, kept, received, keep, send):
    rows = keep.shape[0]
    total = kept[...].astype(F32) + received[...].astype(F32)
    keep[...] = total[:rows].astype(keep.dtype)
    send[...] = total[rows:].astype(send.dtype)


def last_add_body(meta, kept, received, keep, send):
    for out, mine in ((keep, True), (send, False)):
        rows = half_of(meta, keep.shape[0], mine)
        out[...] = (kept[rows, :].astype(F32) + received[rows, :].astype(F32)).astype(out.dtype)


def scale_body(factor, meta, keep, received, out):
    width = keep.shape[1]
    out[:, half_of(meta, width, True)] = keep[...] * factor
    out[:, half_of(meta, width, False)] = received[...].astype(F32) * factor


def cascade_body(counts, meta, *refs):
    keep, send = refs[-2:]
    half = keep.shape[1]
    total = None
    start = 0
    rows = 2 * half >> (len(counts) - 1)
    for count in counts:
        level = lanes(refs[start])[:rows].astype(F32)
        for ref in refs[start + 1 : start + count]:
            level = level + lanes(ref)[:rows].astype(F32)
        start += count
        rows *= 2
        total = level if total is None else level + spread(total, 2, HALF_ROOT)
    put_planes(keep, total[:half])
    put_planes(send, total[half:])


def near_body(meta, keep, recv, dk, dv):
    rows, width = dk.shape[0], keep.shape[2]
    matrix = group_matrix(rows, keep.shape[1] - rows, 2, 1)
    for plane, out in enumerate((dk, dv)):
        own = keep[plane, :rows] + spread(keep[plane, rows:], 2, HALF_ROOT)
        out[:, half_of(meta, width, True)] = own
        other = recv[plane, :rows].astype(F32) + dot(matrix, recv[plane, rows:], NN) * HALF_ROOT
        out[:, half_of(meta, width, False)] = other


def finish_body(meta, base_k, base_v, up_keep, up_recv, dk, dv):
    rows, width = dk.shape[0], up_keep.shape[2]
    times = rows // up_keep.shape[1]
    factor = HALF_ROOT * HALF_ROOT
    matrix = group_matrix(rows, up_recv.shape[1], times, 1)
    mine, theirs = half_of(meta, width, True), half_of(meta, width, False)
    for plane, (base, out) in enumerate(((base_k, dk), (base_v, dv))):
        out[:, mine] = (base[:, mine] + spread(up_keep[plane], times, factor)).astype(BF16)
        received = dot(matrix, up_recv[plane], NN) * factor
        out[:, theirs] = (base[:, theirs] + received).astype(BF16)


def place_body(meta, *refs):
    outs = refs[2 * len(refs) // 3 :]
    for index, out in enumerate(outs):
        width = out.shape[1] // 2
        out[:, half_of(meta, width, True)] = refs[2 * index][...]
        out[:, half_of(meta, width, False)] = refs[2 * index + 1][...]


def body(queries, keys, values, out_weight, out_grad):
    inner = queries.shape[2]
    half = inner // 2
    length = queries.shape[1]
    heads = HEADS // 2
    seq_count = lax.axis_size("seq")
    seq_levels = seq_count.bit_length() - 1
    dp_count = lax.axis_size("dp")
    rank = lax.axis_index("seq")
    bit = rank % 2
    pair = rank // 2
    token_total = length * seq_count * queries.shape[0] * dp_count

    up = [1 << level for level in reversed(range(1, seq_levels))]
    pieces = seq_count // 2

    def halves_of(orders):
        both = [orders, [order[:-2] + order[:-3:-1] for order in orders]]
        masks = [
            [
                [sum(m for s, m in enumerate(order) if index >> s & 1) // 2 for index in range(pieces)]
                for order in one
            ]
            for one in both
        ]
        return [list(zip(*one, strict=True)) for one in both], masks

    stages, masks = halves_of([up[:-2] + [2, 4], [2] + up[:-3] + [4, 8]])
    sum_stages, sum_masks = halves_of([up[:-3] + [4, 8, 2], [2] + up[:-3] + [8, 4]])
    meta = jnp.stack([bit, pair]).astype(jnp.int32)

    query = queries[0]
    key = keys[0]
    value = values[0]
    grad = out_grad[0]
    if dp_count > 1:
        out_weight = lax.all_gather(out_weight, "dp", axis=1, tiled=True)
    cols = out_weight.shape[1] // 2
    piece = 2 * out_weight.shape[0]

    def part(array, which):
        width = array.shape[1] // 2
        return lax.dynamic_slice_in_dim(array, which * width, width, 1)

    q_half = struct(length, half, BF16)
    g_half = struct(length, cols, BF16)
    kv_other = swap(jnp.stack([part(key, 1 - bit), part(value, 1 - bit)]), 1)
    w_theirs = swap(part(out_weight, 1 - bit), 1)
    kv_own = jnp.stack([part(key, bit), part(value, bit)])
    w_mine = part(out_weight, bit)

    sizes = [length // 2, length // 2] + [2 * length >> level for level in range(2, seq_levels + 1)]
    shapes = [planes(rows, half, BF16) for rows in sizes]
    pooled = call(pool_body, meta, (kv_own, kv_other), shapes)
    next_own, next_other = pooled[:2]
    coarse = dict(zip(range(1, seq_levels), pooled[2:], strict=True))

    w_rows = jnp.where(
        bit == 0,
        jnp.concatenate([w_mine, w_theirs], axis=0),
        jnp.concatenate([w_theirs, w_mine], axis=0),
    )
    w_received = permute(w_rows, stages[0][0])
    far_masks = [(h, (1 << h) + (low << 3)) for h in range(3, seq_levels) for low in range(1 << (h - 3))]
    high_parts = [swap(coarse[h], mask) for h, mask in far_masks]
    first_panel = swap(coarse[1], 2)
    w_received, first_panel, *high_parts = lax.optimization_barrier(
        (w_received, first_panel, *high_parts)
    )

    high = jnp.concatenate(high_parts, axis=1)
    second = jnp.concatenate([coarse[2], high], axis=1)
    panels = [high, first_panel, swap(high, 2), swap(second, 4), swap(second, 6)]
    for stage in stages[0][1:-2]:
        w_rows = jnp.concatenate([w_rows, w_received], axis=0)
        w_received = permute(w_rows, stage)
    query, grad = lax.optimization_barrier((query, grad, high))[:2]
    q_other = swap(part(query, 1 - bit), 1)
    g_other = swap(part(grad, 1 - bit), 1)
    q_own = part(query, bit)
    g_own = part(grad, bit)
    n_high, n_second = high.shape[1], coarse[2].shape[1]
    parts = ((1, 0, coarse[1].shape[1]), (3, 0, n_second), (4, 0, n_second))
    parts += ((0, 0, n_high), (2, 0, n_high), (3, n_second, n_high), (4, n_second, n_high))

    w_received = after(w_received, panels[2])
    w_width = cols // 2
    w_rows = [
        jnp.concatenate([rows[:, start : start + w_width] for rows in (w_rows, w_received)], axis=0)
        for start in (0, w_width)
    ]
    w_received = [permute(rows, order[-2]) for rows, order in zip(w_rows, stages, strict=True)]

    key_count = length + length // 2 + sum(rows for _, _, rows in parts)
    att_ops = (q_own, q_other, kv_own, kv_other, next_own, next_other, *panels)
    attn_mine, probs = call(
        lambda *refs: forward_body(parts, *refs),
        after(meta, *w_rows),
        att_ops,
        [struct(2 * length, half, BF16), jax.ShapeDtypeStruct((2 * heads, key_count, length), BF16)],
        flops=32 * 2 * length * key_count * half,
    )

    w_received = lax.optimization_barrier((*w_received, attn_mine))[:2]
    w_rows = [jnp.concatenate(rows, axis=0) for rows in zip(w_rows, w_received, strict=True)]
    w_received = [permute(rows, order[-1]) for rows, order in zip(w_rows, stages, strict=True)]
    quarters = (w_rows[0], w_received[0], w_rows[1], w_received[1])
    attn_theirs = swap(attn_mine, 1)

    scratch = [pltpu.VMEM((pieces * piece, cols), BF16)]
    wg = call(
        lambda *refs: weight_grad_body(piece, sum_masks, *refs),
        meta,
        (attn_mine, attn_theirs, g_own, g_other),
        [struct(pieces * piece // 2, w_width, BF16)] * 4,
        scratch,
    )
    wg_send = lax.optimization_barrier((wg[1], wg[3], *w_received))[:2]
    wg_received = [permute(part, order[-1]) for part, order in zip(wg_send, sum_stages, strict=True)]

    d_keep, d_send = call(
        lambda *refs: d_attn_body(piece, masks, *refs),
        after(meta, wg[0]),
        (g_own, g_other, *quarters),
        [struct(2 * length, half, F32), struct(2 * length, half, BF16)],
        scratch,
    )
    d_recv = swap(d_send, 1)

    back_ops = att_ops + (d_keep, d_recv, probs)

    near_count = length + length // 2
    grad_shapes = [q_half, q_half, planes(near_count, half, F32), planes(near_count, half, BF16)]
    grad_shapes += [planes(p.shape[1], half, BF16) for p in panels]
    grads = call(
        lambda *refs: backward_body(parts, len(panels), *refs),
        meta,
        att_ops + (d_keep, d_recv, probs),
        grad_shapes,
    )
    dq_keep, dq_send, near_keep, near_send, high_own, first_grad, *rest = grads

    back = [swap(part, mask) for part, mask in zip(rest, (2, 4, 6), strict=True)]
    first_back = swap(first_grad, 2)

    def add(kept, received):
        return (kept.astype(F32) + received.astype(F32)).astype(BF16)

    def add_halves(kept, received):
        total = add(kept, received)
        rows = total.shape[0] // 2
        return total[:rows], total[rows:]

    wg_received = lax.optimization_barrier((*wg_received, back[0]))[:2]
    wg_keep, wg_send = zip(*map(add_halves, (wg[0], wg[2]), wg_received), strict=True)
    wg_received = [permute(part, order[-2]) for part, order in zip(wg_send, sum_stages, strict=True)]
    at_meta = after(meta, *wg_send)
    near_recv = swap(near_send, 1)
    dq_recv = swap(dq_send, 1)
    base_k, base_v = call(near_body, meta, (near_keep, near_recv), [struct(length, inner, F32)] * 2)

    at_keep, at_send = call(
        lambda *refs: attended_body(piece, masks, *refs),
        at_meta,
        (attn_mine, attn_theirs, *quarters),
        [g_half, g_half],
        scratch,
    )
    first_back, *others = lax.optimization_barrier(
        (first_back, *back, *wg_received, base_k, base_v, at_keep, dq_recv)
    )
    back, wg_received = others[: len(back)], others[len(back) : len(back) + 2]
    wg_total = jnp.concatenate([add(*both) for both in zip(wg_keep, wg_received, strict=True)], axis=1)
    wg_rows = wg_total.shape[0] // 2
    wg_keep, wg_send = wg_total[:wg_rows], wg_total[wg_rows:]
    wg_received = permute(wg_send, sum_stages[0][-3])
    at_recv = swap(after(at_send, wg_total), 1)
    cuts = [coarse[h].shape[1] for h, _ in far_masks]
    high_shapes = [planes(rows, half, BF16) for rows in cuts]
    high_sums = call(
        lambda *refs: high_body(cuts, (0, n_second, n_second), *refs),
        meta,
        (high_own, *back),
        high_shapes,
    )
    by_level = {1: [first_back], 2: back[1:]}
    high_back = [swap(part, mask) for (_, mask), part in zip(far_masks, high_sums, strict=True)]
    *high_back, wg_received = lax.optimization_barrier((*high_back, wg_received))
    half_rows = struct(piece, cols, BF16)
    wg_keep, wg_send = call(add_body, meta, (wg_keep, wg_received), [half_rows, half_rows])
    wg_received = permute(wg_send, sum_stages[0][-4])
    for (h, _), part in zip(far_masks, high_back, strict=True):
        by_level.setdefault(h, []).append(part)
    levels = list(reversed(range(1, seq_levels)))
    received = [part for h in levels for part in by_level[h]]
    counts = [len(by_level[h]) for h in levels]
    up_rows = coarse[1].shape[1] // 2
    up_keep, up_send = call(
        lambda *refs: cascade_body(counts, *refs),
        after(meta, wg_send),
        received,
        [planes(up_rows, half, F32), planes(up_rows, half, BF16)],
    )
    grad_queries, attended = call(
        place_body,
        after(meta, up_keep),
        (dq_keep, dq_recv, at_keep, at_recv),
        [struct(length, inner, BF16), struct(length, 2 * cols, BF16)],
        last=True,
    )
    wg_received = after(wg_received, up_keep, attended)
    last = (struct(piece // 2, cols, F32), struct(piece // 2, cols, BF16))
    wg_keep, wg_send = call(last_add_body, meta, (wg_keep, wg_received), last)
    (weight_grad,) = call(
        lambda *refs: scale_body(1.0 / math.sqrt(token_total), *refs),
        meta,
        (wg_keep, swap(wg_send, 1)),
        [struct(piece // 2, 2 * cols, F32)],
        last=True,
    )
    if dp_count > 1:
        weight_grad = lax.psum_scatter(
            weight_grad.astype(BF16), "dp", scatter_dimension=1, tiled=True
        ).astype(F32)
    grad_keys, grad_values = call(
        finish_body,
        meta,
        (base_k, base_v, up_keep, swap(up_send, 1)),
        [struct(length, inner, BF16)] * 2,
        last=True,
    )
    return (attended[None], grad_queries[None], grad_keys[None], grad_values[None], weight_grad)


def solution(mesh):
    placed = (
        P("dp", "seq", None),
        P("dp", "seq", None),
        P("dp", "seq", None),
        P("seq", "dp"),
        P("dp", "seq", None),
    )
    return jax.shard_map(
        body,
        mesh=mesh,
        in_specs=placed,
        out_specs=(
            P("dp", "seq", None),
            P("dp", "seq", None),
            P("dp", "seq", None),
            P("dp", "seq", None),
            P("seq", "dp"),
        ),
        check_vma=False,
    )
```
